32 devices in a mesh: dp: 2 (over x), hid: 4 (over y, core), mod: 4 (over z).
Axes of the slice: x: 2, y: 2, z: 4, core: 2. Of those that a mesh axis runs over, the one named last changes fastest.
Arguments:
- tokens: bfloat16 [16928, 768], P(('dp', 'hid', 'mod')), may hold values from -6 to 6
- cotangent: bfloat16 [16928, 768], P(('dp', 'hid', 'mod')), may hold values from -6 to 6
- unit_kind: int32 [32], replicated, may hold values from 0 to 1, as said below
- unit_len: int32 [32, 2], replicated, may hold values from 1 to 529, as said below
- pack_offset: int32 [32], replicated, may hold values from 1 to 529, as said below
- norm1_gain: float32 [768], replicated, may hold values from 0.5 to 1.5
- norm1_bias: float32 [768], replicated, may hold values from -1.8 to 1.8
- qkv_weight: bfloat16 [3, 768, 768], P(None, 'hid'), may hold values from -0.21875 to 0.21875
- out_weight: bfloat16 [768, 768], P('hid'), may hold values from -3 to 3
- norm2_gain: float32 [768], replicated, may hold values from 0.5 to 1.5
- norm2_bias: float32 [768], replicated, may hold values from -1.8 to 1.8
- up_weight: bfloat16 [768, 3072], P('mod', 'hid'), may hold values from -0.21875 to 0.21875
- down_weight: bfloat16 [768, 3072], P('mod', 'hid'), may hold values from -0.109375 to 0.109375
Outputs:
- output: bfloat16 [16928, 768], P(('dp', 'hid', 'mod'))
- tokens_grad: bfloat16 [16928, 768], P(('dp', 'hid', 'mod'))
- norm1_gain_grad: float32 [768], replicated
- norm1_bias_grad: float32 [768], replicated
- qkv_weight_grad: float32 [3, 768, 768], P(None, 'hid')
- out_weight_grad: float32 [768, 768], P('hid')
- norm2_gain_grad: float32 [768], replicated
- norm2_bias_grad: float32 [768], replicated
- up_weight_grad: float32 [768, 3072], P('mod', 'hid')
- down_weight_grad: float32 [768, 3072], P('mod', 'hid')
The draws below stay inside these ranges and needn't reach their ends.
Inputs may be any that keep to these rules, and one draw needn't show every extreme that they name: `unit_kind`: kind 0 is one strip of unit_len[n, 0] patches; kind 1 packs two half strips. `unit_len`: for kind 1 both lengths are at most 264; column 1 is used only for kind 1. For kind 1, unit_len[n, 0] <= pack_offset[n] <= 529 - unit_len[n, 1]; unused for kind 0.
All inputs are finite; a program needn't handle non-finite values.
Results may differ from the reference program's by a relative error of at most 0.012.
The reference program's roundings to bfloat16 on the way count: a program that leaves them out, or rounds other values in their place, can miss the bound.
Values may be sent and summed in bfloat16 or wider, within the bound.
No kernel may reach another device: no remote copies, remote signals or barrier semaphores. Data moves between devices by JAX's collectives and lax.ppermute only.
A program may use at most 192 MiB of HBM per device.

```python
import jax
import jax.numpy as jnp
from jax import lax

D = 768
HEADS = 12
HEAD = 64
FF = 3072
U = 529
HALF = 264
UNITS = 32
TOKENS = 16928
N_DP = 2


def unit_layout(key):
    folded = jax.random.fold_in(key, 11)
    streams = jax.random.split(folded, 7)
    positions = jnp.arange(UNITS, dtype=jnp.int32)
    full_pick = jax.random.randint(streams[0], (), 0, UNITS)
    half_pick = (full_pick + 1 + jax.random.randint(streams[1], (), 0, UNITS - 1)) % UNITS
    unit_kinds = jax.random.randint(streams[2], (UNITS,), 0, 2)
    unit_kinds = jnp.where(positions == full_pick, 0, jnp.where(positions == half_pick, 1, unit_kinds))
    long_lengths = jax.random.randint(streams[3], (UNITS,), HALF, U + 1)
    long_lengths = jnp.where(positions == full_pick, U, long_lengths)
    first_half = jax.random.randint(streams[4], (UNITS,), 1, HALF + 1)
    second_half = jax.random.randint(streams[5], (UNITS,), 1, HALF + 1)
    second_half = jnp.where(positions == half_pick, HALF, second_half)
    leading = jnp.where(unit_kinds == 0, long_lengths, first_half)
    spaces = jnp.maximum(U - leading - second_half, 0) + 1
    offsets = leading + jax.random.randint(streams[6], (UNITS,), 0, spaces)
    return (unit_kinds, jnp.stack([leading, second_half], axis=1), offsets)


def draw_unit_kind(key, part):
    return unit_layout(key)[0].astype(jnp.int32)


def draw_unit_len(key, part):
    return unit_layout(key)[1].astype(jnp.int32)


def draw_pack_offset(key, part):
    return unit_layout(key)[2].astype(jnp.int32)


def shard_levels(rng, dims, cuts, smallest, high):
    factor_of, own = 1.0, jax.random.fold_in(rng, 6)
    for axis_at, parts in cuts:
        heights = jnp.exp(jax.random.uniform(jax.random.fold_in(own, axis_at), (parts,), jnp.float32, smallest / len(cuts), high / len(cuts)))
        factor_of = factor_of * jnp.repeat(heights, dims[axis_at] // parts).reshape([-1 if axis == axis_at else 1 for axis in range(len(dims))])
    return factor_of


def bell_draw(stream_key, dims, deviation, reach, cuts=(), held_as=jnp.bfloat16):
    level = shard_levels(stream_key, dims, cuts, -0.22, 0.18) if cuts else 1.0
    array = jax.random.normal(stream_key, dims, jnp.float32) * deviation * level
    return jnp.minimum(jnp.maximum(array, -reach), reach).astype(held_as)


def setup_inputs(seed: int = 0) -> dict:
    arg_keys = jax.random.split(jax.random.key(seed), 14)
    tokens = bell_draw(arg_keys[0], (TOKENS, D), 1.0, 6.0, ((0, 32),))
    cotangent = bell_draw(arg_keys[1], (TOKENS, D), 1.0, 6.0, ((0, 32),))
    unit_kind = draw_unit_kind(jax.random.fold_in(arg_keys[13], 71), 0)
    unit_len = draw_unit_len(jax.random.fold_in(arg_keys[13], 71), 0)
    pack_offset = draw_pack_offset(jax.random.fold_in(arg_keys[13], 71), 0)
    norm1_gain = jnp.clip(1.0 + 0.1 * jax.random.normal(arg_keys[5], (D,), jnp.float32), 0.5, 1.5)
    norm1_bias = bell_draw(arg_keys[6], (D,), 0.3, 1.8, (), jnp.float32)
    qkv_weight = bell_draw(arg_keys[7], (3, D, D), D ** -0.5, 0.21875, ((1, 4),))
    out_weight = bell_draw(arg_keys[8], (D, D), 4 ** -0.5, 3.0, ((0, 4),))
    norm2_gain = jnp.clip(1.0 + 0.1 * jax.random.normal(arg_keys[9], (D,), jnp.float32), 0.5, 1.5)
    norm2_bias = bell_draw(arg_keys[10], (D,), 0.3, 1.8, (), jnp.float32)
    up_weight = bell_draw(arg_keys[11], (D, FF), D ** -0.5, 0.21875, ((0, 4), (1, 4)))
    down_weight = bell_draw(arg_keys[12], (D, FF), FF ** -0.5, 0.109375, ((0, 4), (1, 4)))
    return {"tokens": tokens, "cotangent": cotangent, "unit_kind": unit_kind, "unit_len": unit_len, "pack_offset": pack_offset, "norm1_gain": norm1_gain, "norm1_bias": norm1_bias, "qkv_weight": qkv_weight, "out_weight": out_weight, "norm2_gain": norm2_gain, "norm2_bias": norm2_bias, "up_weight": up_weight, "down_weight": down_weight}


EPSILON = 1e-06
MASKED = -1000000000.0

@jax.custom_vjp
def low(v):
    return lax.optimization_barrier(v.astype(jnp.bfloat16)).astype(jnp.float32)

@jax.custom_vjp
def low_back(v):
    return v

def low_keep(v):
    return (low(v), None)

def low_pass(kept, grad):
    return (grad,)

def back_keep(v):
    return (v, None)

def back_low(kept, grad):
    return (low(grad),)
low.defvjp(low_keep, low_pass)
low_back.defvjp(back_keep, back_low)

def dot_high(left_rows, right_rows):
    return jnp.dot(left_rows, right_rows, precision=lax.Precision.HIGHEST)

def layer_norm(rows, gain, bias):
    row_mean = lax.optimization_barrier(jnp.mean(rows, axis=1, keepdims=True))
    spread = lax.optimization_barrier(jnp.mean(rows * rows, axis=1, keepdims=True)) - row_mean * row_mean
    return (rows - row_mean) * lax.rsqrt(spread + EPSILON) * gain + bias

def unit_mask(kind_one, lengths, offset):
    position = jnp.arange(U, dtype=jnp.int32)
    start_pos = jnp.where(kind_one == 1, offset, U)
    upper_part = position >= start_pos
    key_valid = jnp.where(upper_part, position - start_pos < lengths[1], position < lengths[0])
    return (upper_part[:, None] == upper_part[None, :]) & key_valid[None, :]

def attend_unit(unit_items):
    joint, kind_one, lengths, offset = unit_items
    queries = joint[:, 0]
    key_heads = joint[:, 1]
    value_heads = joint[:, 2]
    allowed = unit_mask(kind_one, lengths, offset)
    scores = jnp.einsum('qhd,khd->hqk', queries, key_heads, precision=lax.Precision.HIGHEST) * HEAD ** (-0.5)
    scores = low_back(jnp.where(allowed[None], scores, MASKED))
    weights = low(jax.nn.softmax(scores, axis=-1))
    return jnp.einsum('hqk,khd->qhd', weights, value_heads, precision=lax.Precision.HIGHEST)

def encoder_layer(parameters, stream, kinds, lengths, offsets):
    gain_one, bias_one, joint_weight, out_weight, gain_two, bias_two, up_weight, down_weight = parameters
    unit_count = kinds.shape[0]
    normed1 = low(layer_norm(stream, gain_one, bias_one))
    joint_matrix = jnp.transpose(joint_weight, (2, 0, 1)).reshape(D, 3 * D)
    projected = low(low_back(dot_high(normed1, joint_matrix)))
    projected = projected.reshape(unit_count, U, 3, HEADS, HEAD)
    heads_out = lax.map(jax.checkpoint(attend_unit), (projected, kinds, lengths, offsets))
    heads_out = low(low_back(heads_out.reshape(unit_count * U, D)))
    middle = stream + low_back(dot_high(heads_out, out_weight))
    normed2 = low(layer_norm(middle, gain_two, bias_two))
    hidden = low_back(dot_high(normed2, up_weight))
    activated = low(jax.nn.gelu(hidden, approximate=False))
    return middle + dot_high(activated, jnp.transpose(down_weight))

def reference(tokens, cotangent, unit_kind, unit_len, pack_offset, norm1_gain, norm1_bias, qkv_weight, out_weight, norm2_gain, norm2_bias, up_weight, down_weight):
    group_count = N_DP
    group_rows = tokens.shape[0] // group_count
    blocks = tokens.astype(jnp.float32).reshape(group_count, group_rows, D)
    kind_blocks = unit_kind.reshape(group_count, -1)
    length_blocks = unit_len.reshape(group_count, -1, 2)
    offset_blocks = pack_offset.reshape(group_count, -1)
    parameters = (norm1_gain.astype(jnp.float32), norm1_bias.astype(jnp.float32), qkv_weight.astype(jnp.float32), out_weight.astype(jnp.float32), norm2_gain.astype(jnp.float32), norm2_bias.astype(jnp.float32), up_weight.astype(jnp.float32), down_weight.astype(jnp.float32))

    def forward(parameters, blocks):

        def group_block(block_items):
            stream, kinds, lengths, offsets = block_items
            return encoder_layer(parameters, stream, kinds, lengths, offsets)
        return lax.map(jax.checkpoint(group_block), (blocks, kind_blocks, length_blocks, offset_blocks))
    result, pullback = jax.vjp(forward, parameters, blocks)
    gradients, stream_grad = pullback(cotangent.astype(jnp.float32).reshape(result.shape))
    return (result.reshape(tokens.shape).astype(jnp.bfloat16), stream_grad.reshape(tokens.shape).astype(jnp.bfloat16), gradients[0], gradients[1], gradients[2], gradients[3], gradients[4], gradients[5], gradients[6], gradients[7])
```

```python
import functools

import jax
import jax.numpy as jnp
from jax import lax
from jax.experimental import pallas as pl
from jax.experimental.pallas import tpu as pltpu
from jax.sharding import PartitionSpec as P

HEAD = 64
U = 529
ROWS = 544
EPSILON = 1e-06
MASKED = -1000000000.0
SCALE = HEAD**-0.5
F32 = jnp.float32
BF16 = jnp.bfloat16
VMEM = pl.BlockSpec(memory_space=pltpu.VMEM)
SMEM = pl.BlockSpec(memory_space=pltpu.SMEM)


def dot(a, b, ca=1, cb=0):
    return lax.dot_general(a, b, (((ca,), (cb,)), ((), ())), preferred_element_type=F32)


def call(kernel, outs, specs, name, flops, aliases=None):
    nbytes = sum(o.size * o.dtype.itemsize for o in outs)
    return pl.pallas_call(
        kernel,
        out_shape=outs,
        in_specs=specs,
        out_specs=[VMEM] * len(outs),
        input_output_aliases=aliases or {},
        compiler_params=pltpu.CompilerParams(vmem_limit_bytes=50 * 1024 * 1024),
        cost_estimate=pl.CostEstimate(
            flops=int(flops), bytes_accessed=int(3 * nbytes), transcendentals=0
        ),
        name=name,
    )


def shape(*dims, dtype=F32):
    return jax.ShapeDtypeStruct(dims, dtype)


def normed(x):
    mean = jnp.mean(x, axis=1, keepdims=True)
    spread = jnp.mean(x * x, axis=1, keepdims=True) - mean * mean
    inverse = lax.rsqrt(spread + EPSILON)
    return (x - mean) * inverse, inverse


def norm_back(upstream, xhat, inverse, gain):
    scaled = upstream * gain
    first = jnp.mean(scaled, axis=1, keepdims=True)
    second = jnp.mean(scaled * xhat, axis=1, keepdims=True)
    return inverse * (scaled - first - xhat * second)


def ln1_kernel(x_ref, g_ref, b_ref, n_ref):
    xhat, _ = normed(x_ref[...].astype(F32))
    n_ref[...] = (xhat * g_ref[...] + b_ref[...]).astype(BF16)


def allowed_mask(meta_ref):
    kind, first, second, offset = meta_ref[0], meta_ref[1], meta_ref[2], meta_ref[3]
    start = jnp.where(kind == 1, offset, U)
    key = lax.broadcasted_iota(jnp.int32, (ROWS, 1), 0)
    query = lax.broadcasted_iota(jnp.int32, (1, ROWS), 1)
    key_upper = key >= start
    limit = jnp.where(key < U, jnp.where(key_upper, second, first), 0)
    place = jnp.where(key_upper, key - start, key)
    key_code = jnp.where(place < limit, jnp.where(key_upper, 1, 0), 2)
    query_code = jnp.where(query >= start, 1, 0)
    return key_code == query_code


def attn_fwd_kernel(meta_ref, n1_ref, w_ref, proj_ref, ho_ref, lse_ref):
    width = w_ref.shape[0] // 3
    proj = dot(w_ref[...], n1_ref[...], 1, 1)
    proj_ref[0:width, :] = (proj[0:width] * SCALE).astype(BF16)
    proj_ref[width:, :] = proj[width:].astype(BF16)
    allowed = allowed_mask(meta_ref)
    lse_ref[...] = jnp.zeros_like(lse_ref)
    for h in range(width // HEAD):
        q = proj_ref[h * HEAD : (h + 1) * HEAD, :]
        k = proj_ref[width + h * HEAD : width + (h + 1) * HEAD, :]
        v = proj_ref[2 * width + h * HEAD : 2 * width + (h + 1) * HEAD, :]
        s = jnp.where(allowed, dot(k, q, 0, 0), MASKED)
        m = jnp.max(s, axis=0, keepdims=True)
        e = jnp.exp(s - m)
        total = jnp.sum(e, axis=0, keepdims=True)
        p = (e * (1.0 / total)).astype(BF16)
        ho_ref[h * HEAD : (h + 1) * HEAD, :] = dot(v, p, 1, 0).astype(BF16)
        lse_ref[h : h + 1, :] = m + jnp.log(total)


def mid_kernel(tok_ref, cot_ref, g_ref, b_ref, *refs):
    blocks = (len(refs) - 4) // 2
    mid_ref, n2_ref, n2t_ref, cott_ref = refs[2 * blocks :]
    acc = tok_ref[...].astype(F32)
    for j in range(blocks):
        acc += dot(refs[j][...], refs[blocks + j][...], 0, 0)
    mid_ref[...] = acc
    xhat, _ = normed(acc)
    n2 = (xhat * g_ref[...] + b_ref[...]).astype(BF16)
    n2_ref[...] = n2
    n2t_ref[...] = n2.T
    cott_ref[...] = cot_ref[...].T


def ffn_kernel(first, n2_ref, n2t_ref, cot_ref, cott_ref, up_ref, down_ref, *refs):
    if first:
        branch_ref, dn2_ref, grad_ref = refs
    else:
        branch_in, dn2_in, branch_ref, dn2_ref, grad_ref = refs
    d = up_ref.shape[0]
    tile = 256
    for t in range(d // tile):
        cols = slice(t * tile, (t + 1) * tile)
        hidden = dot(n2_ref[...], up_ref[:, cols])
        d_act = dot(cot_ref[...], down_ref[:, cols])
        cdf = 0.5 * (1.0 + lax.erf(hidden * (0.5**0.5)))
        pdf = jnp.exp(-0.5 * hidden * hidden) * 0.3989422804014327
        act = (hidden * cdf).astype(BF16)
        d_hid = (d_act * (cdf + hidden * pdf)).astype(BF16)
        b_part = dot(act, down_ref[:, cols], 1, 1)
        d_part = dot(d_hid, up_ref[:, cols], 1, 1)
        if t == 0:
            if first:
                branch_ref[...] = b_part
                dn2_ref[...] = d_part
            else:
                branch_ref[...] = branch_in[...] + b_part
                dn2_ref[...] = dn2_in[...] + d_part
        else:
            branch_ref[...] += b_part
            dn2_ref[...] += d_part
        grad_ref[0:d, cols] = dot(n2t_ref[...], d_hid).astype(BF16)
        grad_ref[d : 2 * d, cols] = dot(cott_ref[...], act).astype(BF16)


def mid2_kernel(mid_ref, branch_ref, dn2_ref, cot_ref, g_ref, out_ref, dmid_ref, datt_ref, gg_ref, bg_ref):
    mid = mid_ref[...]
    out_ref[...] = (mid + branch_ref[...])[:U].astype(BF16)
    xhat, inverse = normed(mid)
    up = dn2_ref[...]
    dmid = cot_ref[...].astype(F32) + norm_back(up, xhat, inverse, g_ref[...])
    dmid_ref[...] = dmid
    datt_ref[...] = dmid.astype(BF16)
    gg_ref[...] = jnp.sum(up * xhat, axis=0, keepdims=True)
    bg_ref[...] = jnp.sum(up, axis=0, keepdims=True)


def attn_bwd_kernel(first, meta_ref, proj_ref, lse_ref, ho_ref, datt_ref, n1_ref, w_ref, wo_ref, *refs):
    if first:
        dn1_ref, grad_ref, dproj_ref = refs
    else:
        dn1_in, dn1_ref, grad_ref, dproj_ref = refs
    width = wo_ref.shape[0]
    allowed = allowed_mask(meta_ref)
    datt = datt_ref[...]
    dheads = dot(wo_ref[...], datt, 1, 1).astype(BF16)
    grad_ref[3 * width :, :] = dot(ho_ref[...], datt).astype(BF16)
    for h in range(width // HEAD):
        rows = slice(h * HEAD, (h + 1) * HEAD)
        q = proj_ref[h * HEAD : (h + 1) * HEAD, :]
        k = proj_ref[width + h * HEAD : width + (h + 1) * HEAD, :]
        v = proj_ref[2 * width + h * HEAD : 2 * width + (h + 1) * HEAD, :]
        do = dheads[rows]
        s = jnp.where(allowed, dot(k, q, 0, 0), MASKED)
        p = jnp.exp(s - lse_ref[h : h + 1, :])
        dp = dot(v, do, 0, 0)
        delta = jnp.sum(p * dp, axis=0, keepdims=True)
        ds = (p * (dp - delta)).astype(BF16)
        dproj_ref[h * HEAD : (h + 1) * HEAD, :] = (dot(k, ds, 1, 0) * SCALE).astype(BF16)
        dproj_ref[width + h * HEAD : width + (h + 1) * HEAD, :] = dot(q, ds, 1, 1).astype(BF16)
        dproj_ref[2 * width + h * HEAD : 2 * width + (h + 1) * HEAD, :] = dot(
            do, p.astype(BF16), 1, 1
        ).astype(BF16)
    dproj = dproj_ref[...]
    grad_ref[0 : 3 * width, :] = dot(dproj, n1_ref[...]).astype(BF16)
    part = dot(dproj, w_ref[...], 0, 0)
    if first:
        dn1_ref[...] = part
    else:
        dn1_ref[...] = dn1_in[...] + part


def final_kernel(tok_ref, dmid_ref, dn1_ref, g_ref, out_ref, gg_ref, bg_ref):
    xhat, inverse = normed(tok_ref[...].astype(F32))
    up = dn1_ref[...]
    out_ref[...] = (dmid_ref[...] + norm_back(up, xhat, inverse, g_ref[...]))[:U].astype(BF16)
    gg_ref[...] = jnp.sum(up * xhat, axis=0, keepdims=True)
    bg_ref[...] = jnp.sum(up, axis=0, keepdims=True)


def body(
    tokens,
    cotangent,
    unit_kind,
    unit_len,
    pack_offset,
    norm1_gain,
    norm1_bias,
    qkv_weight,
    out_weight,
    norm2_gain,
    norm2_bias,
    up_weight,
    down_weight,
):
    hid = lax.axis_size("hid")
    mod = lax.axis_size("mod")
    d = tokens.shape[1]
    width = out_weight.shape[0]
    unit = (lax.axis_index("dp") * hid + lax.axis_index("hid")) * mod + lax.axis_index("mod")
    meta = jnp.stack(
        [unit_kind[unit], unit_len[unit, 0], unit_len[unit, 1], pack_offset[unit]]
    )
    tok = jnp.pad(tokens, ((0, ROWS - U), (0, 0)))
    cot = jnp.pad(cotangent, ((0, ROWS - U), (0, 0)))
    g1, b1, g2, b2 = (v[None] for v in (norm1_gain, norm1_bias, norm2_gain, norm2_bias))

    qo = jnp.concatenate([qkv_weight.reshape(3 * width, d), out_weight], axis=0)
    qo = lax.all_gather(qo, "hid")
    ff = lax.all_gather(jnp.stack([up_weight, down_weight]), ("hid", "mod"))
    ff = ff.reshape(hid, mod, 2, d // mod, d)
    w = [qo[j, : 3 * width] for j in range(hid)]
    wo = [qo[j, 3 * width :] for j in range(hid)]
    up = [ff[j, :, 0].reshape(d, d) for j in range(hid)]
    down = [ff[j, :, 1].reshape(d, d) for j in range(hid)]

    row = shape(ROWS, d)
    row16 = shape(ROWS, d, dtype=BF16)
    wide16 = shape(d, ROWS, dtype=BF16)
    vec = shape(1, d)
    mm = 2 * ROWS * d * d
    (n1,) = call(ln1_kernel, [row16], [VMEM] * 3, "ln1", 1e7)(tok, g1, b1)
    proj, ho, lse = [], [], []
    for j in range(hid):
        a, b, c = call(
            attn_fwd_kernel,
            [shape(3 * width, ROWS, dtype=BF16), shape(width, ROWS, dtype=BF16), shape(8, ROWS)],
            [SMEM] + [VMEM] * 2,
            "attn_fwd",
            mm,
        )(meta, n1, w[j])
        proj.append(a)
        ho.append(b)
        lse.append(c)
    mid, n2, n2t, cott = call(
        mid_kernel, [row, row16, wide16, wide16], [VMEM] * (4 + 2 * hid), "mid", mm
    )(tok, cot, g2, b2, *ho, *wo)
    state = []
    ffgrads = []
    for j in range(hid):
        branch, dn2, grad = call(
            functools.partial(ffn_kernel, j == 0),
            [row, row, shape(2 * d, d, dtype=BF16)],
            [VMEM] * (6 + len(state)),
            "ffn",
            6 * mm,
            {6: 0, 7: 1} if j else None,
        )(n2, n2t, cot, cott, up[j], down[j], *state)
        state = [branch, dn2]
        ffgrads.append(grad)
    output, dmid, datt, g2g, b2g = call(
        mid2_kernel,
        [shape(U, d, dtype=BF16), row, row16, vec, vec],
        [VMEM] * 5,
        "mid2",
        1e7,
    )(mid, branch, dn2, cot, g2)
    state = []
    qograds = []
    for j in range(hid):
        dn1, grad, _ = call(
            functools.partial(attn_bwd_kernel, j == 0),
            [row, shape(d, d, dtype=BF16), shape(3 * width, ROWS, dtype=BF16)],
            [SMEM] + [VMEM] * (7 + len(state)),
            "attn_bwd",
            3 * mm,
            {8: 0} if j else None,
        )(meta, proj[j], lse[j], ho[j], datt, n1, w[j], wo[j], *state)
        state = [dn1]
        qograds.append(grad)
    tokens_grad, g1g, b1g = call(
        final_kernel, [shape(U, d, dtype=BF16), vec, vec], [VMEM] * 4, "final", 1e7
    )(tok, dmid, dn1, g1)

    ffg = jnp.stack(ffgrads).reshape(hid, 2, mod, d // mod, d).transpose(0, 2, 1, 3, 4)
    ffg = lax.psum_scatter(
        ffg.reshape(hid * mod, 2, d // mod, d), ("hid", "mod"), scatter_dimension=0, tiled=True
    )
    ffg = lax.psum(ffg, "dp")[0].astype(F32)
    qog = lax.psum_scatter(jnp.stack(qograds), "hid", scatter_dimension=0, tiled=True)
    qog = lax.psum(qog, ("dp", "mod"))[0].astype(F32)
    vecs = lax.psum(jnp.concatenate([g1g, b1g, g2g, b2g]), ("dp", "hid", "mod"))
    return (
        output,
        tokens_grad,
        vecs[0],
        vecs[1],
        qog[: 3 * width].reshape(3, width, d),
        qog[3 * width :],
        vecs[2],
        vecs[3],
        ffg[0],
        ffg[1],
    )


def solution(mesh):
    rows = P(("dp", "hid", "mod"), None)
    in_specs = (
        rows,
        rows,
        P(),
        P(),
        P(),
        P(),
        P(),
        P(None, "hid", None),
        P("hid", None),
        P(),
        P(),
        P("mod", "hid"),
        P("mod", "hid"),
    )
    out_specs = (
        rows,
        rows,
        P(),
        P(),
        P(None, "hid", None),
        P("hid", None),
        P(),
        P(),
        P("mod", "hid"),
        P("mod", "hid"),
    )
    return jax.shard_map(body, mesh=mesh, in_specs=in_specs, out_specs=out_specs, check_vma=False)
```

```python
import functools

import jax
import jax.numpy as jnp
from jax import lax
from jax.experimental import pallas as pl
from jax.experimental.pallas import tpu as pltpu
from jax.sharding import PartitionSpec as P

HEAD = 64
U = 529
ROWS = 544
PIECES = 8
LOW = 32
PIECE_ROWS = 32
VECTORS = 8
LIMIT = 16
COST = 1
TILE = 256
EPSILON = 1e-06
MASKED = -1000000000.0
SCALE = HEAD**-0.5
F32 = jnp.float32
BF16 = jnp.bfloat16
VMEM = pl.BlockSpec(memory_space=pltpu.VMEM)
SMEM = pl.BlockSpec(memory_space=pltpu.SMEM)
ANY = pl.BlockSpec(memory_space=pl.ANY)


def dot(a, b, ca=1, cb=0):
    return lax.dot_general(a, b, (((ca,), (cb,)), ((), ())), preferred_element_type=F32)


def shape(*dims, dtype=F32):
    return jax.ShapeDtypeStruct(dims, dtype)


def bf(*dims):
    return shape(*dims, dtype=BF16)


def call(
    kernel, outs, specs, name, cost, after=(), aliases=None, scratch=(), out_specs=None, limit=LIMIT
):
    held = len(after)
    nbytes = sum(o.size * o.dtype.itemsize for o in outs)
    run = pl.pallas_call(
        (lambda *refs: kernel(*refs[held:])) if held else kernel,
        out_shape=outs,
        in_specs=[ANY] * held + specs,
        out_specs=out_specs or [VMEM] * len(outs),
        scratch_shapes=list(scratch),
        input_output_aliases={held + i: o for i, o in (aliases or {}).items()},
        compiler_params=pltpu.CompilerParams(vmem_limit_bytes=limit * 1024 * 1024),
        cost_estimate=pl.CostEstimate(
            flops=int(cost * COST * 1.15e9), bytes_accessed=int(2 * nbytes), transcendentals=0
        ),
        name=name,
    )
    return lambda *args: run(*after, *args)


def normed(x):
    mean = jnp.mean(x, axis=1, keepdims=True)
    spread = jnp.mean(x * x, axis=1, keepdims=True) - mean * mean
    inverse = lax.rsqrt(spread + EPSILON)
    return (x - mean) * inverse, inverse


def norm_back(upstream, xhat, inverse, gain):
    scaled = upstream * gain
    first = jnp.mean(scaled, axis=1, keepdims=True)
    second = jnp.mean(scaled * xhat, axis=1, keepdims=True)
    return inverse * (scaled - first - xhat * second)


def ln1_kernel(x_ref, g_ref, b_ref, n_ref):
    xhat, _ = normed(x_ref[...].astype(F32))
    n_ref[...] = (xhat * g_ref[...] + b_ref[...]).astype(BF16)


def mid_kernel(tok_ref, cot_ref, g_ref, b_ref, *refs):
    blocks = (len(refs) - 4) // 2
    mid_ref, n2_ref, n2t_ref, cott_ref = refs[2 * blocks :]
    acc = tok_ref[...].astype(F32)
    for j in range(blocks):
        width = refs[j].shape[0]
        acc += dot(refs[j][...], refs[blocks + j][0, 3 * width :, :], 0, 0)
    mid_ref[...] = acc
    xhat, _ = normed(acc)
    n2 = (xhat * g_ref[...] + b_ref[...]).astype(BF16)
    n2_ref[...] = n2
    n2t_ref[...] = n2.T
    cott_ref[...] = cot_ref[...].T


def mid2_kernel(
    mid_ref, branch_ref, dn2_ref, cot_ref, g_ref, out_ref, dmid_ref, datt_ref, gg_ref, bg_ref
):
    mid = mid_ref[...]
    out_ref[...] = (mid + branch_ref[...])[:U].astype(BF16)
    xhat, inverse = normed(mid)
    up = dn2_ref[...]
    dmid = cot_ref[...].astype(F32) + norm_back(up, xhat, inverse, g_ref[...])
    dmid_ref[...] = dmid
    datt_ref[...] = dmid.astype(BF16)
    gg_ref[...] = jnp.sum(up * xhat, axis=0, keepdims=True)
    bg_ref[...] = jnp.sum(up, axis=0, keepdims=True)


def final_kernel(tok_ref, dmid_ref, dn1_ref, g_ref, out_ref, gg_ref, bg_ref):
    xhat, inverse = normed(tok_ref[...].astype(F32))
    up = dn1_ref[...]
    out_ref[...] = (dmid_ref[...] + norm_back(up, xhat, inverse, g_ref[...]))[:U].astype(BF16)
    gg_ref[...] = jnp.sum(up * xhat, axis=0, keepdims=True)
    bg_ref[...] = jnp.sum(up, axis=0, keepdims=True)


def allowed_mask(meta_ref):
    kind, first, second, offset = meta_ref[0], meta_ref[1], meta_ref[2], meta_ref[3]
    start = jnp.where(kind == 1, offset, U)
    key = lax.broadcasted_iota(jnp.int32, (ROWS, 1), 0)
    query = lax.broadcasted_iota(jnp.int32, (1, ROWS), 1)
    key_upper = key >= start
    limit = jnp.where(key < U, jnp.where(key_upper, second, first), 0)
    place = jnp.where(key_upper, key - start, key)
    key_code = jnp.where(place < limit, jnp.where(key_upper, 1, 0), 2)
    query_code = jnp.where(query >= start, 1, 0)
    return key_code == query_code


def attn_fwd_kernel(meta_ref, n1_ref, w_ref, proj_ref, ho_ref, lse_ref):
    width = w_ref.shape[1] // 4
    proj = dot(w_ref[0, 0 : 3 * width, :], n1_ref[...], 1, 1)
    proj_ref[0:width, :] = (proj[0:width] * SCALE).astype(BF16)
    proj_ref[width:, :] = proj[width:].astype(BF16)
    allowed = allowed_mask(meta_ref)
    lse_ref[...] = jnp.zeros_like(lse_ref)
    for h in range(width // HEAD):
        q, k, v = (proj_ref[c * width + h * HEAD : c * width + (h + 1) * HEAD, :] for c in range(3))
        s = jnp.where(allowed, dot(k, q, 0, 0), MASKED)
        m = jnp.max(s, axis=0, keepdims=True)
        e = jnp.exp(s - m)
        total = jnp.sum(e, axis=0, keepdims=True)
        p = (e * (1.0 / total)).astype(BF16)
        ho_ref[h * HEAD : (h + 1) * HEAD, :] = dot(v, p, 1, 0).astype(BF16)
        lse_ref[h : h + 1, :] = m + jnp.log(total)


def attn_bwd_kernel(i, first, hid, meta_ref, datt_ref, n1_ref, *refs):
    proj_refs, lse_refs, ho_refs, w_refs = (refs[k * hid : (k + 1) * hid] for k in range(4))
    refs = refs[4 * hid :]
    if not first:
        dn1_in = refs[0]
        refs = refs[1:]
    dn1_ref, keep_ref, send_ref, dproj_ref, w_ref = refs
    width = w_refs[0].shape[1] // 4
    allowed = allowed_mask(meta_ref)
    datt = datt_ref[...]
    for r in range(hid):
        for k in range(3):
            w_ref[(3 * r + k) * HEAD : (3 * r + k + 1) * HEAD, :] = w_refs[r][
                0, k * width + i * HEAD : k * width + (i + 1) * HEAD, :
            ]
    wo = jnp.concatenate(
        [w[0, 3 * width + i * HEAD : 3 * width + (i + 1) * HEAD, :] for w in w_refs]
    )
    ho = jnp.concatenate([h[i * HEAD : (i + 1) * HEAD, :] for h in ho_refs])
    dheads = dot(wo, datt, 1, 1).astype(BF16)
    out_grad = dot(ho, datt).astype(BF16)
    for r in range(hid):
        q, k, v = (
            proj_refs[r][c * width + i * HEAD : c * width + (i + 1) * HEAD, :] for c in range(3)
        )
        do = dheads[r * HEAD : (r + 1) * HEAD]
        s = jnp.where(allowed, dot(k, q, 0, 0), MASKED)
        p = jnp.exp(s - lse_refs[r][i : i + 1, :])
        dp = dot(v, do, 0, 0)
        delta = jnp.sum(p * dp, axis=0, keepdims=True)
        ds = (p * (dp - delta)).astype(BF16)
        base = 3 * r * HEAD
        dproj_ref[base : base + HEAD, :] = (dot(k, ds, 1, 0) * SCALE).astype(BF16)
        dproj_ref[base + HEAD : base + 2 * HEAD, :] = dot(q, ds, 1, 1).astype(BF16)
        dproj_ref[base + 2 * HEAD : base + 3 * HEAD, :] = dot(do, p.astype(BF16), 1, 1).astype(
            BF16
        )
    dproj = dproj_ref[...]
    grad = dot(dproj, n1_ref[...]).astype(BF16)
    for r in range(hid):
        ref = (keep_ref, send_ref)[r % 2]
        ref[r // 2, 0 : 3 * HEAD] = grad[3 * r * HEAD : 3 * (r + 1) * HEAD]
        ref[r // 2, 3 * HEAD :] = out_grad[r * HEAD : (r + 1) * HEAD]
    part = dot(dproj, w_ref[...], 0, 0)
    if first:
        dn1_ref[...] = part
    else:
        dn1_ref[...] = dn1_in[...] + part


def piece_rows(place_ref, p, rows):
    piece = (place_ref[0] ^ (p // 2)) * 2 + (place_ref[1] ^ (p % 2))
    return pl.ds(pl.multiple_of(piece * rows, 16), rows)


def ffn_kernel(at, first, place_ref, n2_ref, n2t_ref, cot_ref, cott_ref, *refs):
    groups, refs = refs[: len(set(g for g, _ in at))], refs[len(set(g for g, _ in at)) :]
    if not first:
        branch_in, dn2_in = refs[:2]
        refs = refs[2:]
    branch_ref, dn2_ref, out_ref, up_ref, down_ref, grad_ref, in_sem, out_sem = refs
    d = up_ref.shape[0]
    part = d // PIECES

    def weights(t):
        cols = pl.ds(t * TILE, TILE)
        return [
            pltpu.make_async_copy(
                groups[at[p][0]].at[at[p][1], k, :, cols],
                (up_ref, down_ref)[k].at[piece_rows(place_ref, p, part), cols],
                in_sem.at[t, 2 * p + k],
            )
            for p in range(PIECES)
            for k in range(2)
        ]

    def results(t):
        cols = pl.ds(t * TILE, TILE)
        return [
            pltpu.make_async_copy(
                grad_ref.at[k, piece_rows(place_ref, p, part), cols],
                out_ref.at[p, k, :, cols],
                out_sem.at[t, 2 * p + k],
            )
            for p in range(PIECES)
            for k in range(2)
        ]

    for t in range(d // TILE):
        for c in weights(t):
            c.start()
    for t in range(d // TILE):
        cols = slice(t * TILE, (t + 1) * TILE)
        for c in weights(t):
            c.wait()
        hidden = dot(n2_ref[...], up_ref[:, cols])
        d_act = dot(cot_ref[...], down_ref[:, cols])
        cdf = 0.5 * (1.0 + lax.erf(hidden * (0.5**0.5)))
        pdf = jnp.exp(-0.5 * hidden * hidden) * 0.3989422804014327
        act = (hidden * cdf).astype(BF16)
        d_hid = (d_act * (cdf + hidden * pdf)).astype(BF16)
        b_part = dot(act, down_ref[:, cols], 1, 1)
        d_part = dot(d_hid, up_ref[:, cols], 1, 1)
        if t == 0:
            if first:
                branch_ref[...] = b_part
                dn2_ref[...] = d_part
            else:
                branch_ref[...] = branch_in[...] + b_part
                dn2_ref[...] = dn2_in[...] + d_part
        else:
            branch_ref[...] += b_part
            dn2_ref[...] += d_part
        grad_ref[0, :, cols] = dot(n2t_ref[...], d_hid).astype(BF16)
        grad_ref[1, :, cols] = dot(cott_ref[...], act).astype(BF16)
        for c in results(t):
            c.start()
    for t in range(d // TILE):
        for c in results(t):
            c.wait()


def both(a, b):
    return (a.astype(F32) + b.astype(F32)).astype(BF16)


def blocks_sum(ref):
    total = ref[0].astype(F32)
    for i in range(1, ref.shape[0]):
        total += ref[i].astype(F32)
    return total


def arrive_kernel(mine_ref, z1_ref, z2_ref, z3_ref, qo_ref, a_ref, b_ref, zs_ref, all_ref):
    a_ref[0] = mine_ref[...]
    a_ref[1] = zs_ref[0] = z1_ref[...]
    b_ref[0] = zs_ref[1] = z2_ref[...]
    b_ref[1] = zs_ref[2] = z3_ref[...]
    all_ref[0] = qo_ref[0]
    part = mine_ref.shape[1]
    for i, ref in enumerate((mine_ref, z1_ref, z2_ref, z3_ref)):
        for k in range(2):
            all_ref[1, (2 * i + k) * part : (2 * i + k + 1) * part, :] = ref[k]


def arrive_more_kernel(rest_ref, xs_ref, y_ref, first_ref, last_ref, all_ref):
    first_ref[0] = all_ref[0] = rest_ref[...]
    last_ref[...] = xs_ref[1:3]
    all_ref[1:4] = xs_ref[...]
    all_ref[4:6] = y_ref[...]


def own_ff_kernel(mine_ref, theirs_ref, low_ref, send_ref, keep_ref):
    for p in range(PIECES):
        low_ref[p] = both(mine_ref[p, :, :LOW], theirs_ref[p, :, :LOW])
        out_ref = (keep_ref, send_ref)[p % 2]
        out_ref[p // 2] = both(mine_ref[p, :, LOW:], theirs_ref[p, :, LOW:])


def ff_mid_kernel(other_ref, other_from, low_ref, low_from, high_ref, send_ref, keep_ref):
    high_ref[...] = both(other_ref[...], other_from[...])
    for p in range(PIECES):
        (keep_ref, send_ref)[p % 2][p // 2] = both(low_ref[p], low_from[p])


def ff_late_kernel(own_ref, own_from, high_from, low_ref, low_from, *outs):
    for z, out_ref in enumerate(outs):
        out_ref[:, :LOW] = both(low_ref[z], low_from[z])
        high = own_ref[z].astype(F32) + own_from[z].astype(F32) + high_from[z].astype(F32)
        out_ref[:, LOW:] = high.astype(BF16)


def total_kernel(*refs):
    total = refs[0][...].astype(F32)
    for ref in refs[1:-1]:
        total += ref[...].astype(F32)
    refs[-1][...] = total.astype(BF16)


def ff_join_kernel(place_ref, mine_ref, theirs_ref, up_ref, down_ref):
    part = mine_ref.shape[1]
    for i, ref in enumerate((mine_ref, theirs_ref)):
        rows = pl.ds(pl.multiple_of((place_ref[1] ^ i) * part, 16), part)
        up_ref[rows, :] = ref[0].astype(F32)
        down_ref[rows, :] = ref[1].astype(F32)


def put_vectors(ref, row, value):
    high = value.astype(BF16)
    ref[row : row + VECTORS, :] = high
    ref[row + VECTORS : row + 2 * VECTORS, :] = (value - high.astype(F32)).astype(BF16)


def get_vectors(ref, row):
    both_parts = ref[row : row + 2 * VECTORS, :].astype(F32)
    return both_parts[:VECTORS] + both_parts[VECTORS:]


def chip_sum_kernel(place_ref, *refs):
    refs, outs = refs[:-4], refs[-4:]
    keeps, theirs = refs[0::2], refs[1::2]
    half = keeps[0].shape[1] // 2
    held = outs[0].shape[0] // half
    for i, ref in enumerate(outs):
        x, y = i // 2, i % 2
        rows = pl.ds(pl.multiple_of((place_ref[1] ^ x) * half, half), half)
        for c in range(held):
            ref[c * half : (c + 1) * half, :] = both(keeps[c][y, rows, :], theirs[c][y, rows, :])
        if len(keeps) > held:
            put_vectors(ref, held * half, keeps[held][...] + theirs[held][...])


def plane_sum_kernel(half, place_ref, *refs):
    parts, outs = refs[:4], refs[4:]
    block = PIECE_ROWS
    held = parts[0].shape[0] // half
    for z, ref in enumerate(outs):
        for c in range(held):
            start = c * half + (place_ref[0] ^ z) * block
            rows = pl.ds(pl.multiple_of(start, block), block)
            total = parts[0][rows, :].astype(F32)
            for part in parts[1:]:
                total += part[rows, :].astype(F32)
            ref[c * block : (c + 1) * block, :] = total.astype(BF16)
        if parts[0].shape[0] > held * half:
            put_vectors(ref, held * block, sum(get_vectors(part, held * half) for part in parts))


def qo_total_kernel(*refs):
    rows = refs[0].shape[0] // PIECE_ROWS * PIECE_ROWS
    if refs[0].shape[0] > rows:
        refs, out_ref, vec_ref = refs[:-2], refs[-2], refs[-1]
        vec_ref[...] = sum(get_vectors(ref, rows) for ref in refs)
    else:
        refs, out_ref = refs[:-1], refs[-1]
    total = refs[0][0:rows, :].astype(F32)
    for ref in refs[1:]:
        total += ref[0:rows, :].astype(F32)
    out_ref[...] = total.astype(BF16)


def stack_kernel(*refs):
    for i, ref in enumerate(refs[:-1]):
        refs[-1][i] = ref[...]


def join_kernel(place_ref, *refs):
    qkv_ref, out_ref, full_ref = refs[-3:]
    width = out_ref.shape[0]
    i = 0
    for mine, theirs in zip(refs[0:-3:2], refs[1:-3:2]):
        for c in range(mine.shape[1] // PIECE_ROWS):
            for x, ref in enumerate((mine, theirs)):
                for z in range(ref.shape[0]):
                    at_z, at_x = place_ref[0] ^ z, place_ref[1] ^ x
                    row = (at_x * 2 + at_z // 2) * width + i * HEAD + at_z % 2 * PIECE_ROWS
                    rows = pl.ds(pl.multiple_of(row, PIECE_ROWS), PIECE_ROWS)
                    full_ref[rows, :] = ref[z, c * PIECE_ROWS : (c + 1) * PIECE_ROWS].astype(F32)
            i += 1
    qkv_ref[...] = full_ref[: 3 * width]
    out_ref[...] = full_ref[3 * width :]


def swap(value, axis, bit):
    count = lax.axis_size(axis)
    return lax.ppermute(value, axis, [(i, i ^ bit) for i in range(count)])


def over_core(value):
    return swap(value, "hid", 1)


def over_y(value):
    return swap(value, "hid", 2)


def over_x(value):
    return swap(value, "dp", 1)


def over_z(value, step):
    return swap(value, "mod", step)


def over_x_and_y(value):
    count, hid = lax.axis_size("dp"), lax.axis_size("hid")
    pairs = [(a * hid + h, (a ^ 1) * hid + (h ^ 2)) for a in range(count) for h in range(hid)]
    return lax.ppermute(value, ("dp", "hid"), pairs)


def over_more(value):
    step = 2
    while step < lax.axis_size("dp"):
        value = both(value, swap(value, "dp", step))
        step *= 2
    return value


def body(
    tokens,
    cotangent,
    unit_kind,
    unit_len,
    pack_offset,
    norm1_gain,
    norm1_bias,
    qkv_weight,
    out_weight,
    norm2_gain,
    norm2_bias,
    up_weight,
    down_weight,
):
    hid = lax.axis_size("hid")
    mod = lax.axis_size("mod")
    d = tokens.shape[1]
    width = out_weight.shape[0]
    z_at, x_at = lax.axis_index("mod"), lax.axis_index("dp") & 1
    unit = (lax.axis_index("dp") * hid + lax.axis_index("hid")) * mod + z_at
    meta = jnp.stack([unit_kind[unit], unit_len[unit, 0], unit_len[unit, 1], pack_offset[unit]])
    place = jnp.stack([z_at, x_at])
    tok = jnp.pad(tokens, ((0, ROWS - U), (0, 0)))
    cot = jnp.pad(cotangent, ((0, ROWS - U), (0, 0)))
    g1, b1, g2, b2 = (v[None] for v in (norm1_gain, norm1_bias, norm2_gain, norm2_bias))
    part = d // PIECES
    shard = jnp.stack([up_weight, down_weight])
    mine = lax.dynamic_slice_in_dim(shard, x_at * part, part, 1)
    rest = lax.dynamic_slice_in_dim(shard, (1 - x_at) * part, part, 1)
    qo = [jnp.concatenate([qkv_weight.reshape(3 * width, d), out_weight])[None]] + [None] * 3

    row, row16, wide16, vec = shape(ROWS, d), bf(ROWS, d), bf(d, ROWS), shape(1, d)

    proj, ho, lse = [], [], []

    def attn_fwd(j, after=()):
        outs = [bf(3 * width, ROWS), bf(width, ROWS), shape(8, ROWS)]
        results = call(attn_fwd_kernel, outs, [SMEM] + [VMEM] * 2, "attn_fwd", 4, after)(
            meta, n1, qo[j]
        )
        for kept, value in zip((proj, ho, lse), results):
            kept.append(value)

    state = []

    def ffn(pieces, after=(), cost=9):
        arrays = list({id(a): a for a, _ in pieces}.values())
        at = tuple((next(i for i, b in enumerate(arrays) if b is a), j) for a, j in pieces)
        *state[:], grad = call(
            functools.partial(ffn_kernel, at, not state),
            [row, row, bf(PIECES, 2, part, d)],
            [SMEM] + [VMEM] * 4 + [ANY] * len(arrays) + [VMEM] * len(state),
            "ffn",
            cost,
            after,
            {5 + len(arrays): 0, 6 + len(arrays): 1} if state else None,
            [
                pltpu.VMEM((d, d), BF16),
                pltpu.VMEM((d, d), BF16),
                pltpu.VMEM((2, d, d), BF16),
                pltpu.SemaphoreType.DMA((d // TILE, 2 * PIECES)),
                pltpu.SemaphoreType.DMA((d // TILE, 2 * PIECES)),
            ],
            [VMEM, VMEM, ANY],
        )(place, n2, n2t, cot, cott, *arrays, *state)
        return grad

    qo[1], qo[2] = over_core(qo[0]), over_y(qo[0])
    z1, z2, z3 = (over_z(mine, z) for z in (1, 2, 3))
    (n1,) = call(ln1_kernel, [row16], [VMEM] * 3, "ln1", 2)(tok, g1, b1)
    attn_fwd(0)
    attn_fwd(1)
    a01, a23, zs, together = call(
        arrive_kernel,
        [bf(2, 2, part, d), bf(2, 2, part, d), bf(3, 2, part, d), bf(2, d, d)],
        [VMEM] * 5,
        "arrive",
        2,
        [ho[1]],
    )(mine, z1, z2, z3, qo[2])
    y01, y23, xs = over_y(a01), over_y(a23), over_x(zs)
    crossed = over_core(together)
    qo[3] = crossed
    attn_fwd(2, [a01])
    attn_fwd(3)
    mid, n2, n2t, cott = call(
        mid_kernel, [row, row16, wide16, wide16], [VMEM] * (4 + 2 * hid), "mid", 5
    )(tok, cot, g2, b2, *ho, *qo)

    a0x, a23x, to_core = call(
        arrive_more_kernel,
        [bf(1, 2, part, d), bf(2, 2, part, d), bf(6, 2, part, d)],
        [VMEM] * 3,
        "arrive_more",
        2,
        [mid],
    )(rest, xs, y01)
    y01x, y23x = over_x(y01), over_y(a23x)
    from_core = over_core(to_core)
    b_own = crossed.reshape(2 * PIECES // 2, 2, part, d)
    f0 = ffn(
        [(a01, 0), (a0x, 0), (a01, 1), (xs, 0), (a23, 0), (xs, 1), (a23, 1), (xs, 2)], [to_core]
    )
    f1 = ffn(
        [
            (b_own, 4),
            (from_core, 0),
            (b_own, 5),
            (from_core, 1),
            (b_own, 6),
            (from_core, 2),
            (b_own, 7),
            (from_core, 3),
        ],
        [y01x, y23],
    )
    c1 = over_core(f1)
    v23, v01x, v23x = over_core(y23), over_core(y01x), over_core(y23x)
    f2 = ffn(
        [(y01, 0), (y01x, 0), (y01, 1), (y01x, 1), (y23, 0), (y23x, 0), (y23, 1), (y23x, 1)],
        cost=30,
    )
    high = bf(mod, 2, part - LOW, d)
    halves = [bf(PIECES, 2, LOW, d), high, high]
    own_low, own_send, own_keep = call(own_ff_kernel, halves, [VMEM] * 2, "own_ff", 2, [f2])(
        f0, c1
    )
    own_from = over_x(own_send)
    f3 = ffn(
        [
            (from_core, 4),
            (v01x, 0),
            (from_core, 5),
            (v01x, 1),
            (v23, 0),
            (v23x, 0),
            (v23, 1),
            (v23x, 1),
        ],
        [own_send],
    )
    c3 = over_core(f3)
    other_low, other_send, other_keep = call(
        own_ff_kernel, halves, [VMEM] * 2, "other_ff", 2
    )(f2, c3)
    low_from, other_from = over_y(other_low), over_x(other_send)
    output, dmid, datt, g2g, b2g = call(
        mid2_kernel,
        [bf(U, d), row, row16, vec, vec],
        [VMEM] * 5,
        "mid2",
        4,
        [other_low, other_send],
    )(mid, *state, cot, g2)

    state = []

    def attn_bwd(i, after=()):
        dn1, keep, send = call(
            functools.partial(attn_bwd_kernel, i, not state, hid),
            [row, bf(2, 4 * HEAD, d), bf(2, 4 * HEAD, d)],
            [SMEM] + [VMEM] * (2 + 4 * hid + len(state)),
            "attn_bwd",
            12,
            after,
            {3 + 4 * hid: 0} if state else None,
            [pltpu.VMEM((3 * hid * HEAD, ROWS), BF16), pltpu.VMEM((3 * hid * HEAD, d), BF16)],
        )(meta, datt, n1, *proj, *lse, *ho, *qo, *state)
        state[:] = [dn1]
        return keep, send

    half = 2 * HEAD

    def plane(chunks, after=(), vectors=()):
        rows = half * len(chunks) + (2 * VECTORS if vectors else 0)
        values = [*sum(chunks, ()), *vectors]
        base, *sends = call(
            chip_sum_kernel, [bf(rows, d)] * 4, [SMEM] + [VMEM] * len(values), "chip_sum", 1, after
        )(place, *values)
        return [base] + [over(v) for over, v in zip((over_y, over_x, over_x_and_y), sends)]

    def scatter(parts, after=()):
        held, more = divmod(parts[0].shape[0], half)
        base, *sends = call(
            functools.partial(plane_sum_kernel, half),
            [bf(held * PIECE_ROWS + more, d)] * mod,
            [SMEM] + [VMEM] * 4,
            "plane_sum",
            1,
            after,
        )(place, *parts)
        return [base] + [over_z(v, z + 1) for z, v in enumerate(sends)]

    def gather(parts, after=()):
        rows = parts[0].shape[0] // PIECE_ROWS * PIECE_ROWS
        outs = [bf(rows, d)]
        if parts[0].shape[0] > rows:
            outs.append(shape(VECTORS, d))
        value, *vectors = call(
            qo_total_kernel, outs, [VMEM] * len(parts), "qo_total", 1, after
        )(*parts)
        value = over_more(value)
        return [value] + [over_z(value, z) for z in range(1, mod)], vectors

    def spread(parts, after=()):
        (mine,) = call(
            stack_kernel, [bf(len(parts), *parts[0].shape)], [VMEM] * len(parts), "stack", 1, after
        )(*parts)
        return [mine, over_x(mine)]

    keep0, send0 = attn_bwd(0)
    d0 = over_core(send0)
    low = bf(mod, 2, LOW, d)
    keep1, send1 = attn_bwd(1)
    d1 = over_core(send1)
    high_send, low_send, low_keep = call(
        ff_mid_kernel, [high, low, low], [VMEM] * 4, "ff_mid", 2, [keep1]
    )(other_keep, other_from, own_low, low_from)
    high_from, low_from = over_y(high_send), over_x(low_send)
    parts0 = plane([(keep0, d0)], [keep1])
    keep2, send2 = attn_bwd(2, [parts0[0], low_send])
    d2 = over_core(send2)
    parts0 = scatter(parts0, [keep2])
    tokens_grad, g1g, b1g = call(
        final_kernel, [bf(U, d), vec, vec], [VMEM] * 4, "final", 4, [parts0[0]]
    )(tok, dmid, *state, g1)
    vectors = jnp.pad(jnp.concatenate([g1g, b1g, g2g, b2g]), ((0, VECTORS - 4), (0, 0)))
    vectors_from = over_core(vectors)
    parts = plane([(keep1, d1), (keep2, d2)], [], [vectors, vectors_from])
    ff_parts = call(
        ff_late_kernel, [bf(2, part, d)] * mod, [VMEM] * 5, "ff_late", 2, [parts[0]]
    )(own_keep, own_from, high_from, low_keep, low_from)
    ff_from = [over_z(v, z + 1) for z, v in enumerate(ff_parts[1:])]
    t0, _ = gather(parts0, [ff_parts[0]])
    parts = scatter(parts, [t0[0]])
    t0 = spread(t0, [parts[0]])
    (ff_total,) = call(total_kernel, [bf(2, part, d)], [VMEM] * mod, "ff_total", 1, [t0[0]])(
        ff_parts[0], *ff_from
    )
    ff_total = over_more(ff_total)
    ff_rest = over_x(ff_total)
    t, vectors = gather(parts, [ff_total])
    t = spread(t)
    up_grad, down_grad = call(
        ff_join_kernel, [shape(2 * part, d)] * 2, [SMEM] + [VMEM] * 2, "ff_join", 1, [t[0]]
    )(place, ff_total, ff_rest)
    qkv_grad, out_grad = call(
        join_kernel,
        [shape(3 * width, d), shape(width, d)],
        [SMEM] + [VMEM] * 4,
        "join",
        2,
        scratch=[pltpu.VMEM((d, d), F32)],
    )(place, *t0, *t)
    (vectors,) = vectors
    return (
        output,
        tokens_grad,
        vectors[0],
        vectors[1],
        qkv_grad.reshape(3, width, d),
        out_grad,
        vectors[2],
        vectors[3],
        up_grad,
        down_grad,
    )


def solution(mesh):
    rows = P(("dp", "hid", "mod"), None)
    in_specs = (
        rows,
        rows,
        P(),
        P(),
        P(),
        P(),
        P(),
        P(None, "hid", None),
        P("hid", None),
        P(),
        P(),
        P("mod", "hid"),
        P("mod", "hid"),
    )
    out_specs = (
        rows,
        rows,
        P(),
        P(),
        P(None, "hid", None),
        P("hid", None),
        P(),
        P(),
        P("mod", "hid"),
        P("mod", "hid"),
    )
    return jax.shard_map(body, mesh=mesh, in_specs=in_specs, out_specs=out_specs, check_vma=False)
```

```python
import functools

import jax
import jax.numpy as jnp
from jax import lax
from jax.experimental import pallas as pl
from jax.experimental.pallas import tpu as pltpu
from jax.sharding import PartitionSpec as P

HEAD = 64
U = 529
ROWS = 544
PIECES = 8
LOW = 32
PIECE_ROWS = 32
VECTORS = 8
LIMIT = 16
TILE = 256
EPSILON = 1e-06
MASKED = -1000000000.0
SCALE = HEAD**-0.5
F32 = jnp.float32
BF16 = jnp.bfloat16
VMEM = pl.BlockSpec(memory_space=pltpu.VMEM)
SMEM = pl.BlockSpec(memory_space=pltpu.SMEM)
ANY = pl.BlockSpec(memory_space=pl.ANY)


def dot(a, b, ca=1, cb=0):
    return lax.dot_general(a, b, (((ca,), (cb,)), ((), ())), preferred_element_type=F32)


def shape(*dims, dtype=F32):
    return jax.ShapeDtypeStruct(dims, dtype)


def bf(*dims):
    return shape(*dims, dtype=BF16)


def call(
    kernel, outs, specs, name, cost, after=(), aliases=None, scratch=(), out_specs=None, limit=LIMIT
):
    held = len(after)
    nbytes = sum(o.size * o.dtype.itemsize for o in outs)
    run = pl.pallas_call(
        (lambda *refs: kernel(*refs[held:])) if held else kernel,
        out_shape=outs,
        in_specs=[ANY] * held + specs,
        out_specs=out_specs or [VMEM] * len(outs),
        scratch_shapes=list(scratch),
        input_output_aliases={held + i: o for i, o in (aliases or {}).items()},
        compiler_params=pltpu.CompilerParams(vmem_limit_bytes=limit * 1024 * 1024),
        cost_estimate=pl.CostEstimate(
            flops=int(cost * 1.15e9), bytes_accessed=int(2 * nbytes), transcendentals=0
        ),
        name=name,
    )
    return lambda *args: run(*after, *args)


def normed(x):
    mean = jnp.mean(x, axis=1, keepdims=True)
    spread = jnp.mean(x * x, axis=1, keepdims=True) - mean * mean
    inverse = lax.rsqrt(spread + EPSILON)
    return (x - mean) * inverse, inverse


def norm_back(upstream, xhat, inverse, gain):
    scaled = upstream * gain
    first = jnp.mean(scaled, axis=1, keepdims=True)
    second = jnp.mean(scaled * xhat, axis=1, keepdims=True)
    return inverse * (scaled - first - xhat * second)


def ln1_kernel(x_ref, g_ref, b_ref, n_ref):
    xhat, _ = normed(x_ref[...].astype(F32))
    n_ref[...] = (xhat * g_ref[...] + b_ref[...]).astype(BF16)


def mid_kernel(tok_ref, cot_ref, g_ref, b_ref, *refs):
    blocks = (len(refs) - 4) // 2
    mid_ref, n2_ref, n2t_ref, cott_ref = refs[2 * blocks :]
    acc = tok_ref[...].astype(F32)
    for j in range(blocks):
        width = refs[j].shape[0]
        acc += dot(refs[j][...], refs[blocks + j][0, 3 * width :, :], 0, 0)
    mid_ref[...] = acc
    xhat, _ = normed(acc)
    n2 = (xhat * g_ref[...] + b_ref[...]).astype(BF16)
    n2_ref[...] = n2
    n2t_ref[...] = n2.T
    cott_ref[...] = cot_ref[...].T


def mid2_kernel(
    mid_ref, branch_ref, dn2_ref, cot_ref, g_ref, out_ref, dmid_ref, datt_ref, gg_ref, bg_ref
):
    mid = mid_ref[...]
    out_ref[...] = (mid + branch_ref[...])[:U].astype(BF16)
    xhat, inverse = normed(mid)
    up = dn2_ref[...]
    dmid = cot_ref[...].astype(F32) + norm_back(up, xhat, inverse, g_ref[...])
    dmid_ref[...] = dmid
    datt_ref[...] = dmid.astype(BF16)
    gg_ref[...] = jnp.sum(up * xhat, axis=0, keepdims=True)
    bg_ref[...] = jnp.sum(up, axis=0, keepdims=True)


def final_kernel(tok_ref, dmid_ref, dn1_ref, g_ref, out_ref, gg_ref, bg_ref):
    xhat, inverse = normed(tok_ref[...].astype(F32))
    up = dn1_ref[...]
    out_ref[...] = (dmid_ref[...] + norm_back(up, xhat, inverse, g_ref[...]))[:U].astype(BF16)
    gg_ref[...] = jnp.sum(up * xhat, axis=0, keepdims=True)
    bg_ref[...] = jnp.sum(up, axis=0, keepdims=True)


def allowed_mask(meta_ref):
    kind, first, second, offset = meta_ref[0], meta_ref[1], meta_ref[2], meta_ref[3]
    start = jnp.where(kind == 1, offset, U)
    key = lax.broadcasted_iota(jnp.int32, (ROWS, 1), 0)
    query = lax.broadcasted_iota(jnp.int32, (1, ROWS), 1)
    key_upper = key >= start
    limit = jnp.where(key < U, jnp.where(key_upper, second, first), 0)
    place = jnp.where(key_upper, key - start, key)
    key_code = jnp.where(place < limit, jnp.where(key_upper, 1, 0), 2)
    query_code = jnp.where(query >= start, 1, 0)
    return key_code == query_code


def attn_fwd_kernel(meta_ref, n1_ref, w_ref, proj_ref, ho_ref, lse_ref):
    width = w_ref.shape[1] // 4
    proj = dot(w_ref[0, 0 : 3 * width, :], n1_ref[...], 1, 1)
    proj_ref[0:width, :] = (proj[0:width] * SCALE).astype(BF16)
    proj_ref[width:, :] = proj[width:].astype(BF16)
    allowed = allowed_mask(meta_ref)
    lse_ref[...] = jnp.zeros_like(lse_ref)
    for h in range(width // HEAD):
        q, k, v = (proj_ref[c * width + h * HEAD : c * width + (h + 1) * HEAD, :] for c in range(3))
        s = jnp.where(allowed, dot(k, q, 0, 0), MASKED)
        m = jnp.max(s, axis=0, keepdims=True)
        e = jnp.exp(s - m)
        total = jnp.sum(e, axis=0, keepdims=True)
        p = (e * (1.0 / total)).astype(BF16)
        ho_ref[h * HEAD : (h + 1) * HEAD, :] = dot(v, p, 1, 0).astype(BF16)
        lse_ref[h : h + 1, :] = m + jnp.log(total)


def attn_bwd_kernel(heads, first, hid, meta_ref, datt_ref, n1_ref, *refs):
    proj_refs, lse_refs, ho_refs, w_refs = (refs[k * hid : (k + 1) * hid] for k in range(4))
    refs = refs[4 * hid :]
    if not first:
        dn1_in = refs[0]
        refs = refs[1:]
    dn1_ref, grad_ref, dproj_ref, w_ref = refs
    width = w_refs[0].shape[1] // 4
    allowed = allowed_mask(meta_ref)
    datt = datt_ref[...]
    for n, (r, i) in enumerate(heads):
        for k in range(3):
            w_ref[(3 * n + k) * HEAD : (3 * n + k + 1) * HEAD, :] = w_refs[r][
                0, k * width + i * HEAD : k * width + (i + 1) * HEAD, :
            ]
    wo = jnp.concatenate(
        [w_refs[r][0, 3 * width + i * HEAD : 3 * width + (i + 1) * HEAD, :] for r, i in heads]
    )
    ho = jnp.concatenate([ho_refs[r][i * HEAD : (i + 1) * HEAD, :] for r, i in heads])
    dheads = dot(wo, datt, 1, 1).astype(BF16)
    out_grad = dot(ho, datt).astype(BF16)
    for n, (r, i) in enumerate(heads):
        q, k, v = (
            proj_refs[r][c * width + i * HEAD : c * width + (i + 1) * HEAD, :] for c in range(3)
        )
        do = dheads[n * HEAD : (n + 1) * HEAD]
        s = jnp.where(allowed, dot(k, q, 0, 0), MASKED)
        p = jnp.exp(s - lse_refs[r][i : i + 1, :])
        dp = dot(v, do, 0, 0)
        delta = jnp.sum(p * dp, axis=0, keepdims=True)
        ds = (p * (dp - delta)).astype(BF16)
        base = 3 * n * HEAD
        dproj_ref[base : base + HEAD, :] = (dot(k, ds, 1, 0) * SCALE).astype(BF16)
        dproj_ref[base + HEAD : base + 2 * HEAD, :] = dot(q, ds, 1, 1).astype(BF16)
        dproj_ref[base + 2 * HEAD : base + 3 * HEAD, :] = dot(do, p.astype(BF16), 1, 1).astype(
            BF16
        )
    dproj = dproj_ref[...]
    grad = dot(dproj, n1_ref[...]).astype(BF16)
    for n, (r, i) in enumerate(heads):
        at = (n // 2, r // 2)
        grad_ref[at[0], at[1], 0 : 3 * HEAD] = grad[3 * n * HEAD : 3 * (n + 1) * HEAD]
        grad_ref[at[0], at[1], 3 * HEAD :] = out_grad[n * HEAD : (n + 1) * HEAD]
    part = dot(dproj, w_ref[...], 0, 0)
    if first:
        dn1_ref[...] = part
    else:
        dn1_ref[...] = dn1_in[...] + part


def piece_rows(place_ref, p, rows):
    piece = (place_ref[0] ^ (p // 2)) * 2 + (place_ref[1] ^ (p % 2))
    return pl.ds(pl.multiple_of(piece * rows, 16), rows)


def ffn_kernel(at, first, place_ref, n2_ref, n2t_ref, cot_ref, cott_ref, *refs):
    groups, refs = refs[: len(set(g for g, _ in at))], refs[len(set(g for g, _ in at)) :]
    if not first:
        branch_in, dn2_in = refs[:2]
        refs = refs[2:]
    branch_ref, dn2_ref, out_ref, up_ref, down_ref, grad_ref, in_sem, out_sem = refs
    d = up_ref.shape[0]
    part = d // PIECES

    def weights(t):
        cols = pl.ds(t * TILE, TILE)
        return [
            pltpu.make_async_copy(
                groups[at[p][0]].at[at[p][1], k, :, cols],
                (up_ref, down_ref)[k].at[piece_rows(place_ref, p, part), cols],
                in_sem.at[t, 2 * p + k],
            )
            for p in range(PIECES)
            for k in range(2)
        ]

    def results(t):
        cols = pl.ds(t * TILE, TILE)
        return [
            pltpu.make_async_copy(
                grad_ref.at[k, piece_rows(place_ref, p, part), cols],
                out_ref.at[p, k, :, cols],
                out_sem.at[t, 2 * p + k],
            )
            for p in range(PIECES)
            for k in range(2)
        ]

    for t in range(d // TILE):
        for c in weights(t):
            c.start()
    for t in range(d // TILE):
        cols = slice(t * TILE, (t + 1) * TILE)
        for c in weights(t):
            c.wait()
        hidden = dot(n2_ref[...], up_ref[:, cols])
        d_act = dot(cot_ref[...], down_ref[:, cols])
        cdf = 0.5 * (1.0 + lax.erf(hidden * (0.5**0.5)))
        pdf = jnp.exp(-0.5 * hidden * hidden) * 0.3989422804014327
        act = (hidden * cdf).astype(BF16)
        d_hid = (d_act * (cdf + hidden * pdf)).astype(BF16)
        b_part = dot(act, down_ref[:, cols], 1, 1)
        d_part = dot(d_hid, up_ref[:, cols], 1, 1)
        if t == 0:
            if first:
                branch_ref[...] = b_part
                dn2_ref[...] = d_part
            else:
                branch_ref[...] = branch_in[...] + b_part
                dn2_ref[...] = dn2_in[...] + d_part
        else:
            branch_ref[...] += b_part
            dn2_ref[...] += d_part
        grad_ref[0, :, cols] = dot(n2t_ref[...], d_hid).astype(BF16)
        grad_ref[1, :, cols] = dot(cott_ref[...], act).astype(BF16)
        for c in results(t):
            c.start()
    for t in range(d // TILE):
        for c in results(t):
            c.wait()


def both(a, b):
    return (a.astype(F32) + b.astype(F32)).astype(BF16)


def blocks_sum(ref):
    total = ref[0].astype(F32)
    for i in range(1, ref.shape[0]):
        total += ref[i].astype(F32)
    return total


def arrive_kernel(mine_ref, z1_ref, z2_ref, z3_ref, qo_ref, a_ref, b_ref, zs_ref, all_ref):
    a_ref[0] = mine_ref[...]
    a_ref[1] = zs_ref[0] = z1_ref[...]
    b_ref[0] = zs_ref[1] = z2_ref[...]
    b_ref[1] = zs_ref[2] = z3_ref[...]
    all_ref[0] = qo_ref[0]
    part = mine_ref.shape[1]
    for i, ref in enumerate((mine_ref, z1_ref, z2_ref, z3_ref)):
        for k in range(2):
            all_ref[1, (2 * i + k) * part : (2 * i + k + 1) * part, :] = ref[k]


def arrive_more_kernel(rest_ref, xs_ref, y_ref, first_ref, last_ref, all_ref):
    first_ref[0] = all_ref[0] = rest_ref[...]
    last_ref[...] = xs_ref[1:3]
    all_ref[1:4] = xs_ref[...]
    all_ref[4:6] = y_ref[...]


def arrive_last_kernel(a_ref, b_ref, c_ref, all_ref):
    for i, ref in enumerate((a_ref, b_ref, c_ref)):
        all_ref[2 * i : 2 * i + 2] = ref[...]


def own_ff_kernel(mine_ref, theirs_ref, low_ref, send_ref, keep_ref):
    for p in range(PIECES):
        low_ref[p] = both(mine_ref[p, :, :LOW], theirs_ref[p, :, :LOW])
        out_ref = (keep_ref, send_ref)[p % 2]
        out_ref[p // 2] = both(mine_ref[p, :, LOW:], theirs_ref[p, :, LOW:])


def cut_pairs(ref, send_ref, keep_ref, other_ref=None):
    for z in range(ref.shape[0]):
        value = ref[z] if other_ref is None else both(ref[z], other_ref[z])
        (keep_ref, send_ref)[z % 2][z // 2] = value


def own_high_kernel(keep_ref, from_ref, zsend_ref, zkeep_ref):
    cut_pairs(keep_ref, zsend_ref, zkeep_ref, from_ref)


def own_mid_kernel(keep_ref, from_ref, near_ref, far_ref):
    near_ref[...] = both(keep_ref[0], from_ref[0])
    far_ref[...] = both(keep_ref[1], from_ref[1])


def ff_mid_kernel(keep_ref, from_ref, low_ref, low_from, send_ref, keep_out):
    high = keep_ref.shape[2]
    for z in range(keep_ref.shape[0]):
        ref = (keep_out, send_ref)[z % 2]
        ref[z // 2, :, :high] = both(keep_ref[z], from_ref[z])
        for x in range(2):
            rows = slice(high + x * LOW, high + (x + 1) * LOW)
            ref[z // 2, :, rows] = both(low_ref[2 * z + x], low_from[2 * z + x])


def ff_last_kernel(near_ref, far_from, share_ref, low_keep, low_send):
    high = share_ref.shape[1]
    total = near_ref[...].astype(F32) + far_from[...].astype(F32)
    share_ref[...] = total[:, :high].astype(BF16)
    low_keep[...] = total[:, high : high + LOW].astype(BF16)
    low_send[...] = total[:, high + LOW :].astype(BF16)


def ff_total_kernel(low_ref, low_from, near_ref, far_from, share_from, out_ref):
    out_ref[:, :LOW] = both(low_ref[...], low_from[...])
    high = near_ref[...].astype(F32) + far_from[...].astype(F32) + share_from[...].astype(F32)
    out_ref[:, LOW:] = high.astype(BF16)


def ff_join_kernel(place_ref, mine_ref, theirs_ref, up_ref, down_ref):
    part = mine_ref.shape[1]
    for i, ref in enumerate((mine_ref, theirs_ref)):
        rows = pl.ds(pl.multiple_of((place_ref[1] ^ i) * part, 16), part)
        up_ref[rows, :] = ref[0].astype(F32)
        down_ref[rows, :] = ref[1].astype(F32)


def put_vectors(ref, row, value):
    high = value.astype(BF16)
    ref[row : row + VECTORS, :] = high
    ref[row + VECTORS : row + 2 * VECTORS, :] = (value - high.astype(F32)).astype(BF16)


def get_vectors(ref, row):
    both_parts = ref[row : row + 2 * VECTORS, :].astype(F32)
    return both_parts[:VECTORS] + both_parts[VECTORS:]


def first_sum_kernel(mine_ref, theirs_ref, own_ref, other_ref):
    for c in range(own_ref.shape[0]):
        own_ref[c] = both(mine_ref[c, 0], theirs_ref[c, 0])
        other_ref[c] = both(mine_ref[c, 1], theirs_ref[c, 1])


def halve_kernel(place_ref, own_ref, from_ref, keep_ref, send_ref):
    half = own_ref.shape[1] // 2
    for c in range(own_ref.shape[0]):
        for x, ref in enumerate((keep_ref, send_ref)):
            rows = pl.ds(pl.multiple_of((place_ref[1] ^ x) * half, half), half)
            ref[c * half : (c + 1) * half, :] = both(own_ref[c, rows, :], from_ref[c, rows, :])


def chip_sum_kernel(chunk, place_ref, vectors_ref, mine_ref, theirs_ref, *outs):
    half = mine_ref.shape[2] // 2
    for i, ref in enumerate(outs):
        x, y = i // 2, i % 2
        rows = pl.ds(pl.multiple_of((place_ref[1] ^ x) * half, half), half)
        ref[0:half, :] = both(mine_ref[0, y, rows, :], theirs_ref[chunk, y, rows, :])
        put_vectors(ref, half, vectors_ref[...])


def plane_sum_kernel(half, place_ref, *refs):
    early, late = refs[:2], refs[2:6]
    block = PIECE_ROWS
    count = early[0].shape[0] // half
    for z, ref in enumerate(refs[6:]):
        for c in range(count + 1):
            start = c % count * half + (place_ref[0] ^ z) * block
            rows = pl.ds(pl.multiple_of(start, block), block)
            total = sum(p[rows, :].astype(F32) for p in (early if c < count else late))
            ref[c * block : (c + 1) * block, :] = total.astype(BF16)
        put_vectors(ref, (count + 1) * block, sum(get_vectors(part, half) for part in late))


def qo_total_kernel(*refs):
    refs, out_ref, vec_ref = refs[:-2], refs[-2], refs[-1]
    rows = out_ref.shape[0]
    vec_ref[...] = sum(get_vectors(ref, rows) for ref in refs)
    out_ref[...] = sum(ref[0:rows, :].astype(F32) for ref in refs).astype(BF16)


def stack_kernel(vectors_ref, *refs):
    *refs, out_ref, vectors_out = refs
    vectors_out[...] = vectors_ref[...]
    for i, ref in enumerate(refs):
        out_ref[i] = ref[...]


def join_kernel(place_ref, mine_ref, mine_x, others_ref, others_x, qkv_ref, out_ref, full_ref):
    width = out_ref.shape[0]
    for x, (first, rest) in enumerate(((mine_ref, others_ref), (mine_x, others_x))):
        for z in range(rest.shape[0] + 1):
            for i in range(first.shape[0] // PIECE_ROWS):
                at_z, at_x = place_ref[0] ^ z, place_ref[1] ^ x
                row = (at_x * 2 + at_z // 2) * width + i * HEAD + at_z % 2 * PIECE_ROWS
                source = rest.at[z - 1] if z else first
                full_ref[pl.ds(pl.multiple_of(row, PIECE_ROWS), PIECE_ROWS), :] = source[
                    i * PIECE_ROWS : (i + 1) * PIECE_ROWS, :
                ].astype(F32)
    qkv_ref[...] = full_ref[: 3 * width]
    out_ref[...] = full_ref[3 * width :]


def swap(value, axis, bit):
    count = lax.axis_size(axis)
    return lax.ppermute(value, axis, [(i, i ^ bit) for i in range(count)])


def over_core(value):
    return swap(value, "hid", 1)


def over_y(value):
    return swap(value, "hid", 2)


def over_x(value):
    return swap(value, "dp", 1)


def over_z(value, step):
    return swap(value, "mod", step)


def over_x_and_y(value):
    count, hid = lax.axis_size("dp"), lax.axis_size("hid")
    pairs = [(a * hid + h, (a ^ 1) * hid + (h ^ 2)) for a in range(count) for h in range(hid)]
    return lax.ppermute(value, ("dp", "hid"), pairs)


def over_more(value):
    step = 2
    while step < lax.axis_size("dp"):
        value = (value.astype(F32) + swap(value, "dp", step).astype(F32)).astype(value.dtype)
        step *= 2
    return value


def body(
    tokens,
    cotangent,
    unit_kind,
    unit_len,
    pack_offset,
    norm1_gain,
    norm1_bias,
    qkv_weight,
    out_weight,
    norm2_gain,
    norm2_bias,
    up_weight,
    down_weight,
):
    hid = lax.axis_size("hid")
    mod = lax.axis_size("mod")
    d = tokens.shape[1]
    width = out_weight.shape[0]
    z_at, x_at = lax.axis_index("mod"), lax.axis_index("dp") & 1
    unit = (lax.axis_index("dp") * hid + lax.axis_index("hid")) * mod + z_at
    meta = jnp.stack([unit_kind[unit], unit_len[unit, 0], unit_len[unit, 1], pack_offset[unit]])
    place = jnp.stack([z_at, x_at])
    tok = jnp.pad(tokens, ((0, ROWS - U), (0, 0)))
    cot = jnp.pad(cotangent, ((0, ROWS - U), (0, 0)))
    g1, b1, g2, b2 = (v[None] for v in (norm1_gain, norm1_bias, norm2_gain, norm2_bias))
    part = d // PIECES
    shard = jnp.stack([up_weight, down_weight])
    mine = lax.dynamic_slice_in_dim(shard, x_at * part, part, 1)
    rest = lax.dynamic_slice_in_dim(shard, (1 - x_at) * part, part, 1)
    qo = [jnp.concatenate([qkv_weight.reshape(3 * width, d), out_weight])[None]] + [None] * 3

    row, row16, wide16, vec = shape(ROWS, d), bf(ROWS, d), bf(d, ROWS), shape(1, d)

    proj, ho, lse = [], [], []

    def attn_fwd(j, after=()):
        outs = [bf(3 * width, ROWS), bf(width, ROWS), shape(8, ROWS)]
        results = call(attn_fwd_kernel, outs, [SMEM] + [VMEM] * 2, "attn_fwd", 2.4, after)(
            meta, n1, qo[j]
        )
        for kept, value in zip((proj, ho, lse), results):
            kept.append(value)

    state = []

    def ffn(pieces, after=(), cost=5.4):
        arrays = list({id(a): a for a, _ in pieces}.values())
        at = tuple((next(i for i, b in enumerate(arrays) if b is a), j) for a, j in pieces)
        *state[:], grad = call(
            functools.partial(ffn_kernel, at, not state),
            [row, row, bf(PIECES, 2, part, d)],
            [SMEM] + [VMEM] * 4 + [ANY] * len(arrays) + [VMEM] * len(state),
            "ffn",
            cost,
            after,
            {5 + len(arrays): 0, 6 + len(arrays): 1} if state else None,
            [
                pltpu.VMEM((d, d), BF16),
                pltpu.VMEM((d, d), BF16),
                pltpu.VMEM((2, d, d), BF16),
                pltpu.SemaphoreType.DMA((d // TILE, 2 * PIECES)),
                pltpu.SemaphoreType.DMA((d // TILE, 2 * PIECES)),
            ],
            [VMEM, VMEM, ANY],
        )(place, n2, n2t, cot, cott, *arrays, *state)
        return grad

    qo[1], qo[2] = over_core(qo[0]), over_y(qo[0])
    z1, z2, z3 = (over_z(mine, z) for z in (1, 2, 3))
    (n1,) = call(ln1_kernel, [row16], [VMEM] * 3, "ln1", 2)(tok, g1, b1)
    attn_fwd(0)
    attn_fwd(1)
    a01, a23, zs, together = call(
        arrive_kernel,
        [bf(2, 2, part, d), bf(2, 2, part, d), bf(3, 2, part, d), bf(2, d, d)],
        [VMEM] * 5,
        "arrive",
        2,
        [ho[0], ho[1]],
    )(mine, z1, z2, z3, qo[2])
    y01, y23, xs = over_y(a01), over_y(a23), over_x(zs)
    crossed = over_core(together)
    qo[3] = crossed
    attn_fwd(2, [a01])
    attn_fwd(3)
    mid, n2, n2t, cott = call(
        mid_kernel, [row, row16, wide16, wide16], [VMEM] * (4 + 2 * hid), "mid", 3
    )(tok, cot, g2, b2, *ho, *qo)

    a0x, a23x, to_core = call(
        arrive_more_kernel,
        [bf(1, 2, part, d), bf(2, 2, part, d), bf(6, 2, part, d)],
        [VMEM] * 3,
        "arrive_more",
        2,
        [mid],
    )(rest, xs, y01)
    y01x, y23x = over_x(y01), over_y(a23x)
    from_core = over_core(to_core)
    b_own = crossed.reshape(2 * PIECES // 2, 2, part, d)
    f0 = ffn(
        [(a01, 0), (a0x, 0), (a01, 1), (xs, 0), (a23, 0), (xs, 1), (a23, 1), (xs, 2)], [to_core]
    )
    f1 = ffn(
        [
            (b_own, 4),
            (from_core, 0),
            (b_own, 5),
            (from_core, 1),
            (b_own, 6),
            (from_core, 2),
            (b_own, 7),
            (from_core, 3),
        ],
        [y01x, y23],
    )
    c1 = over_core(f1)
    (to_core,) = call(arrive_last_kernel, [bf(6, 2, part, d)], [VMEM] * 3, "arrive_last", 25, [f1])(
        y01x, y23, y23x
    )
    last = over_core(to_core)
    high = bf(mod, 2, part - LOW, d)
    halves = [bf(PIECES, 2, LOW, d), high, high]
    own_low, own_send, own_keep = call(
        own_ff_kernel, halves, [VMEM] * 2, "own_ff", 25, [to_core]
    )(f0, c1)
    own_from = over_x(own_send)
    f3 = ffn(
        [
            (from_core, 4),
            (last, 0),
            (from_core, 5),
            (last, 1),
            (last, 2),
            (last, 4),
            (last, 3),
            (last, 5),
        ],
        [own_send],
    )
    c3 = over_core(f3)
    f2 = ffn(
        [(y01, 0), (y01x, 0), (y01, 1), (y01x, 1), (y23, 0), (y23x, 0), (y23, 1), (y23x, 1)],
        cost=60,
    )
    other_low, other_send, other_keep = call(
        own_ff_kernel, halves, [VMEM] * 2, "other_ff", 2
    )(f2, c3)
    low_from, other_from = over_y(other_low), over_x(other_send)
    output, dmid, datt, g2g, b2g = call(
        mid2_kernel,
        [bf(U, d), row, row16, vec, vec],
        [VMEM] * 5,
        "mid2",
        1,
        [other_low, other_send],
    )(mid, *state, cot, g2)

    state = []

    def attn_bwd(heads, cost, after=()):
        rows = 3 * HEAD * len(heads)
        dn1, grad = call(
            functools.partial(attn_bwd_kernel, heads, not state, hid),
            [row, bf(len(heads) // 2, 2, 4 * HEAD, d)],
            [SMEM] + [VMEM] * (2 + 4 * hid + len(state)),
            "attn_bwd",
            cost,
            after,
            {3 + 4 * hid: 0} if state else None,
            [pltpu.VMEM((rows, ROWS), BF16), pltpu.VMEM((rows, d), BF16)],
        )(meta, datt, n1, *proj, *lse, *ho, *qo, *state)
        state[:] = [dn1]
        return grad

    def stage(kernel, name, outs, *arrays, after=(), first=VMEM, cost=10):
        return call(kernel, outs, [first] + [VMEM] * (len(arrays) - 1), name, cost, after)(*arrays)

    def gather(parts, after=()):
        rows = parts[0].shape[0] // PIECE_ROWS * PIECE_ROWS
        outs = [bf(rows, d), shape(VECTORS, d)]
        value, vectors = call(
            qo_total_kernel, outs, [VMEM] * len(parts), "qo_total", 1, after
        )(*parts)
        value = over_more(value)
        return value, over_x(value), [over_z(value, z) for z in range(1, mod)], vectors

    rows = part - LOW
    half, extra = 2 * HEAD, 2 * VECTORS
    own_z, own_keep = stage(
        own_high_kernel,
        "own_high",
        [bf(mod // 2, 2, rows, d)] * 2,
        own_keep,
        own_from,
        after=[datt],
        cost=1,
    )
    own_zfrom = over_z(own_z, 1)
    count = width // HEAD
    theirs = attn_bwd([(r, i) for i in range(count) for r in (1, 3)], 20, [own_z])
    theirs = over_core(theirs)
    own_near, own_far = stage(
        own_mid_kernel, "own_mid", [bf(2, rows, d)] * 2, own_keep, own_zfrom, after=state, cost=1
    )
    own_far = over_z(own_far, 2)
    early = attn_bwd([(r, i) for i in range(count - 1) for r in (0, 2)], 60)
    own_early, other_early = stage(
        first_sum_kernel,
        "first_sum",
        [bf(count - 1, 4 * HEAD, d)] * 2,
        early,
        theirs,
    )
    early_from = over_y(other_early)
    zsend, zkeep = stage(
        ff_mid_kernel,
        "ff_mid",
        [bf(mod // 2, 2, rows + 2 * LOW, d)] * 2,
        other_keep,
        other_from,
        own_low,
        low_from,
        after=[own_early],
    )
    zfrom = over_z(zsend, 1)
    late = attn_bwd([(r, count - 1) for r in (0, 2)], 12, [zsend])
    tokens_grad, g1g, b1g = call(
        final_kernel, [bf(U, d), vec, vec], [VMEM] * 4, "final", 15, [late, own_far]
    )(tok, dmid, *state, g1)
    vectors = jnp.pad(jnp.concatenate([g1g, b1g, g2g, b2g]), ((0, VECTORS - 4), (0, 0)))
    base, *sends = stage(
        functools.partial(chip_sum_kernel, count - 1),
        "chip_sum",
        [bf(half + extra, d)] * 4,
        place,
        vectors,
        late,
        theirs,
        first=SMEM,
    )
    late = [base] + [over(v) for over, v in zip((over_y, over_x, over_x_and_y), sends)]
    early, send = stage(
        halve_kernel,
        "halve",
        [bf((count - 1) * half, d)] * 2,
        place,
        own_early,
        early_from,
        after=[base],
        first=SMEM,
    )
    early_from = over_x(send)
    near, far = stage(
        own_mid_kernel, "ff_late", [bf(2, rows + 2 * LOW, d)] * 2, zkeep, zfrom, after=[send]
    )
    far = over_z(far, 2)
    base, *sends = stage(
        functools.partial(plane_sum_kernel, half),
        "plane_sum",
        [bf(count * PIECE_ROWS + extra, d)] * mod,
        place,
        early,
        early_from,
        *late,
        after=[near],
        first=SMEM,
        cost=20,
    )
    parts = [base] + [over_z(v, z + 1) for z, v in enumerate(sends)]
    share, low_keep, low_send = stage(
        ff_last_kernel, "ff_last", [bf(2, rows, d)] + [bf(2, LOW, d)] * 2, near, far, after=[base]
    )
    share_from, low_from = over_y(share), over_x(low_send)
    mine, vectors = stage(
        qo_total_kernel,
        "qo_total",
        [bf(count * PIECE_ROWS, d), shape(VECTORS, d)],
        *parts,
        after=[share],
    )
    mine = over_more(mine)
    vectors = over_more(vectors)
    mine_x, others = over_x(mine), [over_z(mine, z) for z in range(1, mod)]
    (ff_total,) = stage(
        ff_total_kernel,
        "ff_total",
        [bf(2, part, d)],
        low_keep,
        low_from,
        own_near,
        own_far,
        share_from,
        after=[mine],
    )
    ff_total = over_more(ff_total)
    ff_rest = over_x(ff_total)
    others, vectors = stage(
        stack_kernel,
        "stack",
        [bf(mod - 1, *mine.shape), shape(VECTORS, d)],
        vectors,
        *others,
        after=[ff_total, mine_x],
    )
    others_x = over_x(others)
    vectors = vectors + over_core(vectors)
    up_grad, down_grad = stage(
        ff_join_kernel,
        "ff_join",
        [shape(2 * part, d)] * 2,
        place,
        ff_total,
        ff_rest,
        after=[others],
        first=SMEM,
    )
    qkv_grad, out_grad = call(
        join_kernel,
        [shape(3 * width, d), shape(width, d)],
        [SMEM] + [VMEM] * 4,
        "join",
        2,
        scratch=[pltpu.VMEM((d, d), F32)],
    )(place, mine, mine_x, others, others_x)
    return (
        output,
        tokens_grad,
        vectors[0],
        vectors[1],
        qkv_grad.reshape(3, width, d),
        out_grad,
        vectors[2],
        vectors[3],
        up_grad,
        down_grad,
    )


def solution(mesh):
    rows = P(("dp", "hid", "mod"), None)
    in_specs = (
        rows,
        rows,
        P(),
        P(),
        P(),
        P(),
        P(),
        P(None, "hid", None),
        P("hid", None),
        P(),
        P(),
        P("mod", "hid"),
        P("mod", "hid"),
    )
    out_specs = (
        rows,
        rows,
        P(),
        P(),
        P(None, "hid", None),
        P("hid", None),
        P(),
        P(),
        P("mod", "hid"),
        P("mod", "hid"),
    )
    return jax.shard_map(body, mesh=mesh, in_specs=in_specs, out_specs=out_specs, check_vma=False)
```

```python
import functools

import jax
import jax.numpy as jnp
from jax import lax
from jax.experimental import pallas as pl
from jax.experimental.pallas import tpu as pltpu
from jax.sharding import PartitionSpec as P

HEAD = 64
U = 529
ROWS = 544
PIECES = 8
LOW = 32
PIECE_ROWS = 32
VECTORS = 8
LIMIT = 16
TILE = 256
EPSILON = 1e-06
MASKED = -1000000000.0
SCALE = HEAD**-0.5
F32 = jnp.float32
BF16 = jnp.bfloat16
VMEM = pl.BlockSpec(memory_space=pltpu.VMEM)
SMEM = pl.BlockSpec(memory_space=pltpu.SMEM)
ANY = pl.BlockSpec(memory_space=pl.ANY)


def dot(a, b, ca=1, cb=0):
    return lax.dot_general(a, b, (((ca,), (cb,)), ((), ())), preferred_element_type=F32)


def shape(*dims, dtype=F32):
    return jax.ShapeDtypeStruct(dims, dtype)


def bf(*dims):
    return shape(*dims, dtype=BF16)


def call(
    kernel, outs, specs, name, cost, after=(), aliases=None, scratch=(), out_specs=None, limit=LIMIT
):
    held = len(after)
    nbytes = sum(o.size * o.dtype.itemsize for o in outs)
    run = pl.pallas_call(
        (lambda *refs: kernel(*refs[held:])) if held else kernel,
        out_shape=outs,
        in_specs=[ANY] * held + specs,
        out_specs=out_specs or [VMEM] * len(outs),
        scratch_shapes=list(scratch),
        input_output_aliases={held + i: o for i, o in (aliases or {}).items()},
        compiler_params=pltpu.CompilerParams(vmem_limit_bytes=limit * 1024 * 1024),
        cost_estimate=pl.CostEstimate(
            flops=int(cost * 1.15e9), bytes_accessed=int(2 * nbytes), transcendentals=0
        ),
        name=name,
    )
    return lambda *args: run(*after, *args)


def normed(x):
    mean = jnp.mean(x, axis=1, keepdims=True)
    spread = jnp.mean(x * x, axis=1, keepdims=True) - mean * mean
    inverse = lax.rsqrt(spread + EPSILON)
    return (x - mean) * inverse, inverse


def norm_back(upstream, xhat, inverse, gain):
    scaled = upstream * gain
    first = jnp.mean(scaled, axis=1, keepdims=True)
    second = jnp.mean(scaled * xhat, axis=1, keepdims=True)
    return inverse * (scaled - first - xhat * second)


def ln1_kernel(x_ref, g_ref, b_ref, n_ref):
    xhat, _ = normed(x_ref[...].astype(F32))
    n_ref[...] = (xhat * g_ref[...] + b_ref[...]).astype(BF16)


def mid_kernel(tok_ref, cot_ref, g_ref, b_ref, *refs):
    blocks = (len(refs) - 4) // 2
    mid_ref, n2_ref, n2t_ref, cott_ref = refs[2 * blocks :]
    acc = tok_ref[...].astype(F32)
    for j in range(blocks):
        width = refs[j].shape[0]
        acc += dot(refs[j][...], refs[blocks + j][0, 3 * width :, :], 0, 0)
    mid_ref[...] = acc
    xhat, _ = normed(acc)
    n2 = (xhat * g_ref[...] + b_ref[...]).astype(BF16)
    n2_ref[...] = n2
    n2t_ref[...] = n2.T
    cott_ref[...] = cot_ref[...].T


def mid2_kernel(
    mid_ref, branch_ref, dn2_ref, cot_ref, g_ref, out_ref, dmid_ref, datt_ref, gg_ref, bg_ref
):
    mid = mid_ref[...]
    out_ref[...] = (mid + branch_ref[...])[:U].astype(BF16)
    xhat, inverse = normed(mid)
    up = dn2_ref[...]
    dmid = cot_ref[...].astype(F32) + norm_back(up, xhat, inverse, g_ref[...])
    dmid_ref[...] = dmid
    datt_ref[...] = dmid.astype(BF16)
    gg_ref[...] = jnp.sum(up * xhat, axis=0, keepdims=True)
    bg_ref[...] = jnp.sum(up, axis=0, keepdims=True)


def final_kernel(tok_ref, dmid_ref, dn1_ref, g_ref, out_ref, gg_ref, bg_ref):
    xhat, inverse = normed(tok_ref[...].astype(F32))
    up = dn1_ref[...]
    out_ref[...] = (dmid_ref[...] + norm_back(up, xhat, inverse, g_ref[...]))[:U].astype(BF16)
    gg_ref[...] = jnp.sum(up * xhat, axis=0, keepdims=True)
    bg_ref[...] = jnp.sum(up, axis=0, keepdims=True)


def allowed_mask(place_ref, kind_ref, len_ref, offset_ref):
    unit = place_ref[2]
    kind, first, second, offset = kind_ref[unit], len_ref[unit, 0], len_ref[unit, 1], offset_ref[unit]
    start = jnp.where(kind == 1, offset, U)
    key = lax.broadcasted_iota(jnp.int32, (ROWS, 1), 0)
    query = lax.broadcasted_iota(jnp.int32, (1, ROWS), 1)
    key_upper = key >= start
    limit = jnp.where(key < U, jnp.where(key_upper, second, first), 0)
    place = jnp.where(key_upper, key - start, key)
    key_code = jnp.where(place < limit, jnp.where(key_upper, 1, 0), 2)
    query_code = jnp.where(query >= start, 1, 0)
    return key_code == query_code


def attn_fwd_kernel(place_ref, kind_ref, len_ref, offset_ref, n1_ref, w_ref, proj_ref, ho_ref, lse_ref):
    width = w_ref.shape[1] // 4
    proj = dot(w_ref[0, 0 : 3 * width, :], n1_ref[...], 1, 1)
    proj_ref[0:width, :] = (proj[0:width] * SCALE).astype(BF16)
    proj_ref[width:, :] = proj[width:].astype(BF16)
    allowed = allowed_mask(place_ref, kind_ref, len_ref, offset_ref)
    lse_ref[...] = jnp.zeros_like(lse_ref)
    for h in range(width // HEAD):
        q, k, v = (proj_ref[c * width + h * HEAD : c * width + (h + 1) * HEAD, :] for c in range(3))
        s = jnp.where(allowed, dot(k, q, 0, 0), MASKED)
        m = jnp.max(s, axis=0, keepdims=True)
        e = jnp.exp(s - m)
        total = jnp.sum(e, axis=0, keepdims=True)
        p = (e * (1.0 / total)).astype(BF16)
        ho_ref[h * HEAD : (h + 1) * HEAD, :] = dot(v, p, 1, 0).astype(BF16)
        lse_ref[h : h + 1, :] = m + jnp.log(total)


def attn_bwd_kernel(
    heads, first, hid, place_ref, kind_ref, len_ref, offset_ref, datt_ref, n1_ref, *refs
):
    proj_refs, lse_refs, ho_refs, w_refs = (refs[k * hid : (k + 1) * hid] for k in range(4))
    refs = refs[4 * hid :]
    if not first:
        dn1_in = refs[0]
        refs = refs[1:]
    dn1_ref, grad_ref, dproj_ref, w_ref = refs
    width = w_refs[0].shape[1] // 4
    allowed = allowed_mask(place_ref, kind_ref, len_ref, offset_ref)
    datt = datt_ref[...]
    for n, (r, i) in enumerate(heads):
        for k in range(3):
            w_ref[(3 * n + k) * HEAD : (3 * n + k + 1) * HEAD, :] = w_refs[r][
                0, k * width + i * HEAD : k * width + (i + 1) * HEAD, :
            ]
    wo = jnp.concatenate(
        [w_refs[r][0, 3 * width + i * HEAD : 3 * width + (i + 1) * HEAD, :] for r, i in heads]
    )
    ho = jnp.concatenate([ho_refs[r][i * HEAD : (i + 1) * HEAD, :] for r, i in heads])
    dheads = dot(wo, datt, 1, 1).astype(BF16)
    out_grad = dot(ho, datt).astype(BF16)
    for n, (r, i) in enumerate(heads):
        q, k, v = (
            proj_refs[r][c * width + i * HEAD : c * width + (i + 1) * HEAD, :] for c in range(3)
        )
        do = dheads[n * HEAD : (n + 1) * HEAD]
        s = jnp.where(allowed, dot(k, q, 0, 0), MASKED)
        p = jnp.exp(s - lse_refs[r][i : i + 1, :])
        dp = dot(v, do, 0, 0)
        delta = jnp.sum(p * dp, axis=0, keepdims=True)
        ds = (p * (dp - delta)).astype(BF16)
        base = 3 * n * HEAD
        dproj_ref[base : base + HEAD, :] = (dot(k, ds, 1, 0) * SCALE).astype(BF16)
        dproj_ref[base + HEAD : base + 2 * HEAD, :] = dot(q, ds, 1, 1).astype(BF16)
        dproj_ref[base + 2 * HEAD : base + 3 * HEAD, :] = dot(do, p.astype(BF16), 1, 1).astype(
            BF16
        )
    dproj = dproj_ref[...]
    grad = dot(dproj, n1_ref[...]).astype(BF16)
    for n, (r, i) in enumerate(heads):
        at = (n // 2, r // 2)
        grad_ref[at[0], at[1], 0 : 3 * HEAD] = grad[3 * n * HEAD : 3 * (n + 1) * HEAD]
        grad_ref[at[0], at[1], 3 * HEAD :] = out_grad[n * HEAD : (n + 1) * HEAD]
    part = dot(dproj, w_ref[...], 0, 0)
    if first:
        dn1_ref[...] = part
    else:
        dn1_ref[...] = dn1_in[...] + part


def piece_rows(place_ref, p, rows):
    piece = (place_ref[0] ^ (p // 2)) * 2 + (place_ref[1] ^ (p % 2))
    return pl.ds(pl.multiple_of(piece * rows, 16), rows)


def ffn_kernel(at, first, place_ref, n2_ref, n2t_ref, cot_ref, cott_ref, *refs):
    groups, refs = refs[: len(set(g for g, _ in at))], refs[len(set(g for g, _ in at)) :]
    if not first:
        branch_in, dn2_in = refs[:2]
        refs = refs[2:]
    branch_ref, dn2_ref, out_ref, up_ref, down_ref, grad_ref, in_sem, out_sem = refs
    d = up_ref.shape[0]
    part = d // PIECES

    def weights(t):
        cols = pl.ds(t * TILE, TILE)
        return [
            pltpu.make_async_copy(
                groups[at[p][0]].at[at[p][1], k, :, cols],
                (up_ref, down_ref)[k].at[piece_rows(place_ref, p, part), cols],
                in_sem.at[t, 2 * p + k],
            )
            for p in range(PIECES)
            for k in range(2)
        ]

    def results(t):
        cols = pl.ds(t * TILE, TILE)
        return [
            pltpu.make_async_copy(
                grad_ref.at[k, piece_rows(place_ref, p, part), cols],
                out_ref.at[p, k, :, cols],
                out_sem.at[t, 2 * p + k],
            )
            for p in range(PIECES)
            for k in range(2)
        ]

    for t in range(d // TILE):
        for c in weights(t):
            c.start()
    for t in range(d // TILE):
        cols = slice(t * TILE, (t + 1) * TILE)
        for c in weights(t):
            c.wait()
        hidden = dot(n2_ref[...], up_ref[:, cols])
        d_act = dot(cot_ref[...], down_ref[:, cols])
        cdf = 0.5 * (1.0 + lax.erf(hidden * (0.5**0.5)))
        pdf = jnp.exp(-0.5 * hidden * hidden) * 0.3989422804014327
        act = (hidden * cdf).astype(BF16)
        d_hid = (d_act * (cdf + hidden * pdf)).astype(BF16)
        b_part = dot(act, down_ref[:, cols], 1, 1)
        d_part = dot(d_hid, up_ref[:, cols], 1, 1)
        if t == 0:
            if first:
                branch_ref[...] = b_part
                dn2_ref[...] = d_part
            else:
                branch_ref[...] = branch_in[...] + b_part
                dn2_ref[...] = dn2_in[...] + d_part
        else:
            branch_ref[...] += b_part
            dn2_ref[...] += d_part
        grad_ref[0, :, cols] = dot(n2t_ref[...], d_hid).astype(BF16)
        grad_ref[1, :, cols] = dot(cott_ref[...], act).astype(BF16)
        for c in results(t):
            c.start()
    for t in range(d // TILE):
        for c in results(t):
            c.wait()


def both(a, b):
    return (a.astype(F32) + b.astype(F32)).astype(BF16)


def blocks_sum(ref):
    total = ref[0].astype(F32)
    for i in range(1, ref.shape[0]):
        total += ref[i].astype(F32)
    return total


def arrive_first_kernel(qo_ref, shared_ref, z_ref, qo_out, out_ref):
    qo_out[...] = qo_ref[...]
    out_ref[0] = shared_ref[...]
    part = z_ref.shape[1]
    for k in range(2):
        out_ref[1, k * part : (k + 1) * part, :] = z_ref[k]


def pair_kernel(a_ref, b_ref, out_ref):
    out_ref[0] = a_ref[...]
    out_ref[1] = b_ref[...]


def arrive_kernel(
    place_ref, a_ref, z2_ref, z3_ref, plain_ref, shared_ref, shared_x, b_ref, all_ref
):
    b_ref[0] = z2_ref[...]
    b_ref[1] = z3_ref[...]
    part = z2_ref.shape[1]
    for i in range(4):
        for k in range(2):
            rows = slice((2 * i + k) * part, (2 * i + k + 1) * part)
            all_ref[1, rows, :] = a_ref[i, k] if i < 2 else (z2_ref, z3_ref)[i - 2][k]
    plain = plain_ref.shape[0]
    share = shared_ref.shape[0]
    all_ref[0, :plain] = plain_ref[...]
    for i, value in enumerate((shared_ref[...], shared_x[0])):
        start = plain + (place_ref[1] ^ i) * share
        all_ref[0, pl.ds(pl.multiple_of(start, share), share), :] = value


def arrive_more_kernel(rest_ref, first_x, xs_ref, y_ref, all_ref, xs_out, y_out):
    part = rest_ref.shape[1]
    all_ref[0] = rest_ref[...]
    for k in range(2):
        all_ref[1, k] = first_x[1, k * part : (k + 1) * part, :]
    all_ref[2:4] = xs_out[...] = xs_ref[...]
    all_ref[4:6] = y_out[...] = y_ref[...]


def arrive_last_kernel(a_ref, b_ref, c_ref, all_ref):
    for i, ref in enumerate((a_ref, b_ref, c_ref)):
        all_ref[2 * i : 2 * i + 2] = ref[...]


def own_ff_kernel(mine_ref, theirs_ref, low_ref, send_ref, keep_ref):
    for p in range(PIECES):
        low_ref[p] = both(mine_ref[p, :, :LOW], theirs_ref[p, :, :LOW])
        out_ref = (keep_ref, send_ref)[p % 2]
        out_ref[p // 2] = both(mine_ref[p, :, LOW:], theirs_ref[p, :, LOW:])


def cut_pairs(ref, send_ref, keep_ref, other_ref=None):
    for z in range(ref.shape[0]):
        value = ref[z] if other_ref is None else both(ref[z], other_ref[z])
        (keep_ref, send_ref)[z % 2][z // 2] = value


def own_high_kernel(keep_ref, from_ref, zsend_ref, zkeep_ref):
    cut_pairs(keep_ref, zsend_ref, zkeep_ref, from_ref)


def own_mid_kernel(keep_ref, from_ref, near_ref, far_ref):
    near_ref[...] = both(keep_ref[0], from_ref[0])
    far_ref[...] = both(keep_ref[1], from_ref[1])


def ff_mid_kernel(keep_ref, from_ref, low_ref, low_from, send_ref, keep_out):
    high = keep_ref.shape[2]
    for z in range(keep_ref.shape[0]):
        ref = (keep_out, send_ref)[z % 2]
        ref[z // 2, :, :high] = both(keep_ref[z], from_ref[z])
        for x in range(2):
            rows = slice(high + x * LOW, high + (x + 1) * LOW)
            ref[z // 2, :, rows] = both(low_ref[2 * z + x], low_from[2 * z + x])


def ff_last_kernel(near_ref, far_from, share_ref, low_keep, low_send):
    high = share_ref.shape[1]
    total = near_ref[...].astype(F32) + far_from[...].astype(F32)
    share_ref[...] = total[:, :high].astype(BF16)
    low_keep[...] = total[:, high : high + LOW].astype(BF16)
    low_send[...] = total[:, high + LOW :].astype(BF16)


def ff_total_kernel(low_ref, low_from, near_ref, far_from, share_from, out_ref):
    out_ref[:, :LOW] = both(low_ref[...], low_from[...])
    high = near_ref[...].astype(F32) + far_from[...].astype(F32) + share_from[...].astype(F32)
    out_ref[:, LOW:] = high.astype(BF16)


def ff_join_kernel(place_ref, mine_ref, theirs_ref, up_ref, down_ref):
    part = mine_ref.shape[1]
    for i, ref in enumerate((mine_ref, theirs_ref)):
        rows = pl.ds(pl.multiple_of((place_ref[1] ^ i) * part, 16), part)
        up_ref[rows, :] = ref[0].astype(F32)
        down_ref[rows, :] = ref[1].astype(F32)


def put_vectors(ref, row, value):
    high = value.astype(BF16)
    ref[row : row + VECTORS, :] = high
    ref[row + VECTORS : row + 2 * VECTORS, :] = (value - high.astype(F32)).astype(BF16)


def get_vectors(ref, row):
    both_parts = ref[row : row + 2 * VECTORS, :].astype(F32)
    return both_parts[:VECTORS] + both_parts[VECTORS:]


def first_sum_kernel(mine_ref, theirs_ref, own_ref, other_ref):
    for c in range(own_ref.shape[0]):
        own_ref[c] = both(mine_ref[c, 0], theirs_ref[c, 0])
        other_ref[c] = both(mine_ref[c, 1], theirs_ref[c, 1])


def halve_kernel(place_ref, own_ref, from_ref, keep_ref, send_ref):
    half = own_ref.shape[1] // 2
    for c in range(own_ref.shape[0]):
        for x, ref in enumerate((keep_ref, send_ref)):
            rows = pl.ds(pl.multiple_of((place_ref[1] ^ x) * half, half), half)
            ref[c * half : (c + 1) * half, :] = both(own_ref[c, rows, :], from_ref[c, rows, :])


def chip_sum_kernel(chunk, place_ref, vectors_ref, mine_ref, theirs_ref, *outs):
    half = mine_ref.shape[2] // 2
    for i, ref in enumerate(outs):
        x, y = i // 2, i % 2
        rows = pl.ds(pl.multiple_of((place_ref[1] ^ x) * half, half), half)
        ref[0:half, :] = both(mine_ref[0, y, rows, :], theirs_ref[chunk, y, rows, :])
        put_vectors(ref, half, vectors_ref[...])


def plane_sum_kernel(half, place_ref, *refs):
    early, late = refs[:2], refs[2:6]
    block = PIECE_ROWS
    count = early[0].shape[0] // half
    for z, ref in enumerate(refs[6:]):
        for c in range(count + 1):
            start = c % count * half + (place_ref[0] ^ z) * block
            rows = pl.ds(pl.multiple_of(start, block), block)
            total = sum(p[rows, :].astype(F32) for p in (early if c < count else late))
            ref[c * block : (c + 1) * block, :] = total.astype(BF16)
        put_vectors(ref, (count + 1) * block, sum(get_vectors(part, half) for part in late))


def qo_total_kernel(*refs):
    refs, out_ref, vec_ref = refs[:-2], refs[-2], refs[-1]
    rows = out_ref.shape[0]
    vec_ref[...] = sum(get_vectors(ref, rows) for ref in refs)
    out_ref[...] = sum(ref[0:rows, :].astype(F32) for ref in refs).astype(BF16)


def stack_kernel(vectors_ref, *refs):
    *refs, out_ref, vectors_out = refs
    vectors_out[...] = vectors_ref[...]
    for i, ref in enumerate(refs):
        out_ref[i] = ref[...]


def join_kernel(place_ref, mine_ref, mine_x, others_ref, others_x, qkv_ref, out_ref, full_ref):
    width = out_ref.shape[0]
    for x, (first, rest) in enumerate(((mine_ref, others_ref), (mine_x, others_x))):
        for z in range(rest.shape[0] + 1):
            for i in range(first.shape[0] // PIECE_ROWS):
                at_z, at_x = place_ref[0] ^ z, place_ref[1] ^ x
                row = (at_x * 2 + at_z // 2) * width + i * HEAD + at_z % 2 * PIECE_ROWS
                source = rest.at[z - 1] if z else first
                full_ref[pl.ds(pl.multiple_of(row, PIECE_ROWS), PIECE_ROWS), :] = source[
                    i * PIECE_ROWS : (i + 1) * PIECE_ROWS, :
                ].astype(F32)
    qkv_ref[...] = full_ref[: 3 * width]
    out_ref[...] = full_ref[3 * width :]


def swap(value, axis, bit):
    count = lax.axis_size(axis)
    return lax.ppermute(value, axis, [(i, i ^ bit) for i in range(count)])


def over_core(value):
    return swap(value, "hid", 1)


def over_y(value):
    return swap(value, "hid", 2)


def over_x(value):
    return swap(value, "dp", 1)


def over_z(value, step):
    return swap(value, "mod", step)


def over_x_and_y(value):
    count, hid = lax.axis_size("dp"), lax.axis_size("hid")
    pairs = [(a * hid + h, (a ^ 1) * hid + (h ^ 2)) for a in range(count) for h in range(hid)]
    return lax.ppermute(value, ("dp", "hid"), pairs)


def over_more(value):
    step = 2
    while step < lax.axis_size("dp"):
        value = (value.astype(F32) + swap(value, "dp", step).astype(F32)).astype(value.dtype)
        step *= 2
    return value


def body(
    tokens,
    cotangent,
    unit_kind,
    unit_len,
    pack_offset,
    norm1_gain,
    norm1_bias,
    qkv_weight,
    out_weight,
    norm2_gain,
    norm2_bias,
    up_weight,
    down_weight,
):
    hid = lax.axis_size("hid")
    mod = lax.axis_size("mod")
    d = tokens.shape[1]
    width = out_weight.shape[0]
    z_at, x_at = lax.axis_index("mod"), lax.axis_index("dp") & 1
    unit = (lax.axis_index("dp") * hid + lax.axis_index("hid")) * mod + z_at
    place = jnp.stack([z_at, x_at, unit])
    meta = (place, unit_kind, unit_len, pack_offset)
    tok = jnp.pad(tokens, ((0, ROWS - U), (0, 0)))
    cot = jnp.pad(cotangent, ((0, ROWS - U), (0, 0)))
    g1, b1, g2, b2 = (v[None] for v in (norm1_gain, norm1_bias, norm2_gain, norm2_bias))
    part = d // PIECES
    shard = jnp.stack([up_weight, down_weight])
    mine = lax.dynamic_slice_in_dim(shard, x_at * part, part, 1)
    rest = lax.dynamic_slice_in_dim(shard, (1 - x_at) * part, part, 1)
    qo = [jnp.concatenate([qkv_weight.reshape(3 * width, d), out_weight])[None]] + [None] * 3

    row, row16, wide16, vec = shape(ROWS, d), bf(ROWS, d), bf(d, ROWS), shape(1, d)

    proj, ho, lse = [], [], []

    def attn_fwd(j, cost, after=()):
        outs = [bf(3 * width, ROWS), bf(width, ROWS), shape(8, ROWS)]
        results = call(attn_fwd_kernel, outs, [SMEM] * 4 + [VMEM] * 2, "attn_fwd", cost, after)(
            *meta, n1, qo[j]
        )
        for kept, value in zip((proj, ho, lse), results):
            kept.append(value)

    state = []

    def ffn(pieces, after=(), cost=5.4):
        arrays = list({id(a): a for a, _ in pieces}.values())
        at = tuple((next(i for i, b in enumerate(arrays) if b is a), j) for a, j in pieces)
        *state[:], grad = call(
            functools.partial(ffn_kernel, at, not state),
            [row, row, bf(PIECES, 2, part, d)],
            [SMEM] + [VMEM] * 4 + [ANY] * len(arrays) + [VMEM] * len(state),
            "ffn",
            cost,
            after,
            {5 + len(arrays): 0, 6 + len(arrays): 1} if state else None,
            [
                pltpu.VMEM((d, d), BF16),
                pltpu.VMEM((d, d), BF16),
                pltpu.VMEM((2, d, d), BF16),
                pltpu.SemaphoreType.DMA((d // TILE, 2 * PIECES)),
                pltpu.SemaphoreType.DMA((d // TILE, 2 * PIECES)),
            ],
            [VMEM, VMEM, ANY],
        )(place, n2, n2t, cot, cott, *arrays, *state)
        return grad

    qkv_rows = qkv_weight.reshape(3 * width, d)
    shared_y = over_y(jnp.where(x_at == 0, qkv_weight[2], out_weight))
    plain_y = over_y(qkv_rows[: 2 * width])
    z1, z2, z3 = (over_z(mine, z) for z in (1, 2, 3))
    (n1,) = call(ln1_kernel, [row16], [VMEM] * 3, "ln1", 2)(tok, g1, b1)
    to_core, first = call(
        arrive_first_kernel,
        [bf(1, d, d), bf(2, width, d)],
        [VMEM] * 3,
        "arrive_first",
        1,
        [n1],
    )(qo[0], shared_y, z1)
    first_x, qo[1] = over_x(first), over_core(to_core)
    attn_fwd(0, 60, [first])
    attn_fwd(1, 60)
    (a01,) = call(pair_kernel, [bf(2, 2, part, d)], [VMEM] * 2, "pair", 1, [ho[0], ho[1]])(mine, z1)
    y01 = over_y(a01)
    a23, together = call(
        arrive_kernel,
        [bf(2, 2, part, d), bf(2, d, d)],
        [SMEM] + [VMEM] * 6,
        "arrive",
        2,
    )(place, a01, z2, z3, plain_y, shared_y, first_x)
    y23, xs = over_y(a23), over_x(a23)
    qo[2], qo[3] = together, over_core(together)
    attn_fwd(2, 60)
    attn_fwd(3, 2.4)
    mid, n2, n2t, cott = call(
        mid_kernel, [row, row16, wide16, wide16], [VMEM] * (4 + 2 * hid), "mid", 3
    )(tok, cot, g2, b2, *ho, *qo)

    to_core, xs_again, y01_again = call(
        arrive_more_kernel,
        [bf(6, 2, part, d), bf(2, 2, part, d), bf(2, 2, part, d)],
        [VMEM] * 4,
        "arrive_more",
        2,
        [mid],
    )(rest, first_x, xs, y01)
    y01x, y23x = over_x(y01_again), over_y(xs_again)
    from_core = over_core(to_core)
    b_own = qo[3].reshape(PIECES, 2, part, d)
    first_x = first_x.reshape(2, 2, part, d)
    rest = rest[None]
    f0 = ffn(
        [
            (a01, 0),
            (rest, 0),
            (a01, 1),
            (first_x, 1),
            (a23, 0),
            (xs, 0),
            (a23, 1),
            (xs, 1),
        ],
        [to_core],
        cost=60,
    )
    f1 = ffn(
        [
            (b_own, 4),
            (from_core, 0),
            (b_own, 5),
            (from_core, 1),
            (b_own, 6),
            (from_core, 2),
            (b_own, 7),
            (from_core, 3),
        ],
    )
    c1 = over_core(f1)
    (to_core,) = call(arrive_last_kernel, [bf(6, 2, part, d)], [VMEM] * 3, "arrive_last", 60, [f1])(
        y01x, y23, y23x
    )
    last = over_core(to_core)
    high = bf(mod, 2, part - LOW, d)
    halves = [bf(PIECES, 2, LOW, d), high, high]
    own_low, own_send, own_keep = call(
        own_ff_kernel, halves, [VMEM] * 2, "own_ff", 25, [to_core]
    )(f0, c1)
    own_from = over_x(own_send)
    f3 = ffn(
        [
            (from_core, 4),
            (last, 0),
            (from_core, 5),
            (last, 1),
            (last, 2),
            (last, 4),
            (last, 3),
            (last, 5),
        ],
        [own_send],
    )
    c3 = over_core(f3)
    f2 = ffn(
        [(y01, 0), (y01x, 0), (y01, 1), (y01x, 1), (y23, 0), (y23x, 0), (y23, 1), (y23x, 1)],
        cost=60,
    )
    other_low, other_send, other_keep = call(
        own_ff_kernel, halves, [VMEM] * 2, "other_ff", 2
    )(f2, c3)
    low_from, other_from = over_y(other_low), over_x(other_send)
    output, dmid, datt, g2g, b2g = call(
        mid2_kernel,
        [bf(U, d), row, row16, vec, vec],
        [VMEM] * 5,
        "mid2",
        1,
        [other_low, other_send],
    )(mid, *state, cot, g2)

    state = []

    def attn_bwd(heads, cost, after=()):
        rows = 3 * HEAD * len(heads)
        dn1, grad = call(
            functools.partial(attn_bwd_kernel, heads, not state, hid),
            [row, bf(len(heads) // 2, 2, 4 * HEAD, d)],
            [SMEM] * 4 + [VMEM] * (2 + 4 * hid + len(state)),
            "attn_bwd",
            cost,
            after,
            {6 + 4 * hid: 0} if state else None,
            [pltpu.VMEM((rows, ROWS), BF16), pltpu.VMEM((rows, d), BF16)],
        )(*meta, datt, n1, *proj, *lse, *ho, *qo, *state)
        state[:] = [dn1]
        return grad

    def stage(kernel, name, outs, *arrays, after=(), first=VMEM, cost=10):
        return call(kernel, outs, [first] + [VMEM] * (len(arrays) - 1), name, cost, after)(*arrays)

    def gather(parts, after=()):
        rows = parts[0].shape[0] // PIECE_ROWS * PIECE_ROWS
        outs = [bf(rows, d), shape(VECTORS, d)]
        value, vectors = call(
            qo_total_kernel, outs, [VMEM] * len(parts), "qo_total", 1, after
        )(*parts)
        value = over_more(value)
        return value, over_x(value), [over_z(value, z) for z in range(1, mod)], vectors

    rows = part - LOW
    half, extra = 2 * HEAD, 2 * VECTORS
    own_z, own_keep = stage(
        own_high_kernel,
        "own_high",
        [bf(mod // 2, 2, rows, d)] * 2,
        own_keep,
        own_from,
        after=[datt],
        cost=1,
    )
    own_zfrom = over_z(own_z, 1)
    count = width // HEAD
    theirs = attn_bwd([(r, i) for i in range(count) for r in (1, 3)], 20, [own_z])
    theirs = over_core(theirs)
    own_near, own_far = stage(
        own_mid_kernel, "own_mid", [bf(2, rows, d)] * 2, own_keep, own_zfrom, after=state, cost=1
    )
    own_far = over_z(own_far, 2)
    early = attn_bwd([(r, i) for i in range(count - 1) for r in (0, 2)], 60)
    own_early, other_early = stage(
        first_sum_kernel,
        "first_sum",
        [bf(count - 1, 4 * HEAD, d)] * 2,
        early,
        theirs,
    )
    early_from = over_y(other_early)
    zsend, zkeep = stage(
        ff_mid_kernel,
        "ff_mid",
        [bf(mod // 2, 2, rows + 2 * LOW, d)] * 2,
        other_keep,
        other_from,
        own_low,
        low_from,
        after=[own_early],
    )
    zfrom = over_z(zsend, 1)
    late = attn_bwd([(r, count - 1) for r in (0, 2)], 12, [zsend])
    tokens_grad, g1g, b1g = call(
        final_kernel, [bf(U, d), vec, vec], [VMEM] * 4, "final", 15, [late, own_far]
    )(tok, dmid, *state, g1)
    vectors = jnp.pad(jnp.concatenate([g1g, b1g, g2g, b2g]), ((0, VECTORS - 4), (0, 0)))
    base, *sends = stage(
        functools.partial(chip_sum_kernel, count - 1),
        "chip_sum",
        [bf(half + extra, d)] * 4,
        place,
        vectors,
        late,
        theirs,
        first=SMEM,
    )
    late = [base] + [over(v) for over, v in zip((over_y, over_x, over_x_and_y), sends)]
    early, send = stage(
        halve_kernel,
        "halve",
        [bf((count - 1) * half, d)] * 2,
        place,
        own_early,
        early_from,
        after=[base],
        first=SMEM,
    )
    early_from = over_x(send)
    near, far = stage(
        own_mid_kernel, "ff_late", [bf(2, rows + 2 * LOW, d)] * 2, zkeep, zfrom, after=[send]
    )
    far = over_z(far, 2)
    base, *sends = stage(
        functools.partial(plane_sum_kernel, half),
        "plane_sum",
        [bf(count * PIECE_ROWS + extra, d)] * mod,
        place,
        early,
        early_from,
        *late,
        after=[near],
        first=SMEM,
        cost=20,
    )
    parts = [base] + [over_z(v, z + 1) for z, v in enumerate(sends)]
    share, low_keep, low_send = stage(
        ff_last_kernel, "ff_last", [bf(2, rows, d)] + [bf(2, LOW, d)] * 2, near, far, after=[base]
    )
    share_from, low_from = over_y(share), over_x(low_send)
    mine, vectors = stage(
        qo_total_kernel,
        "qo_total",
        [bf(count * PIECE_ROWS, d), shape(VECTORS, d)],
        *parts,
        after=[share],
    )
    mine = over_more(mine)
    vectors = over_more(vectors)
    mine_x, others = over_x(mine), [over_z(mine, z) for z in range(1, mod)]
    (ff_total,) = stage(
        ff_total_kernel,
        "ff_total",
        [bf(2, part, d)],
        low_keep,
        low_from,
        own_near,
        own_far,
        share_from,
        after=[mine],
    )
    ff_total = over_more(ff_total)
    ff_rest = over_x(ff_total)
    others, vectors = stage(
        stack_kernel,
        "stack",
        [bf(mod - 1, *mine.shape), shape(VECTORS, d)],
        vectors,
        *others,
        after=[ff_total, mine_x],
    )
    others_x = over_x(others)
    vectors = vectors + over_core(vectors)
    up_grad, down_grad = stage(
        ff_join_kernel,
        "ff_join",
        [shape(2 * part, d)] * 2,
        place,
        ff_total,
        ff_rest,
        after=[others],
        first=SMEM,
    )
    qkv_grad, out_grad = call(
        join_kernel,
        [shape(3 * width, d), shape(width, d)],
        [SMEM] + [VMEM] * 4,
        "join",
        2,
        scratch=[pltpu.VMEM((d, d), F32)],
    )(place, mine, mine_x, others, others_x)
    return (
        output,
        tokens_grad,
        vectors[0],
        vectors[1],
        qkv_grad.reshape(3, width, d),
        out_grad,
        vectors[2],
        vectors[3],
        up_grad,
        down_grad,
    )


def solution(mesh):
    rows = P(("dp", "hid", "mod"), None)
    in_specs = (
        rows,
        rows,
        P(),
        P(),
        P(),
        P(),
        P(),
        P(None, "hid", None),
        P("hid", None),
        P(),
        P(),
        P("mod", "hid"),
        P("mod", "hid"),
    )
    out_specs = (
        rows,
        rows,
        P(),
        P(),
        P(None, "hid", None),
        P("hid", None),
        P(),
        P(),
        P("mod", "hid"),
        P("mod", "hid"),
    )
    return jax.shard_map(body, mesh=mesh, in_specs=in_specs, out_specs=out_specs, check_vma=False)
```

```python
import functools

import jax
import jax.numpy as jnp
from jax import lax
from jax.experimental import pallas as pl
from jax.experimental.pallas import tpu as pltpu
from jax.sharding import PartitionSpec as P

HEAD = 64
U = 529
ROWS = 544
PIECES = 8
LOW = 32
PIECE_ROWS = 32
VECTORS = 8
LIMIT = 16
TILE = 256
EPSILON = 1e-06
MASKED = -1000000000.0
SCALE = HEAD**-0.5
F32 = jnp.float32
BF16 = jnp.bfloat16
VMEM = pl.BlockSpec(memory_space=pltpu.VMEM)
SMEM = pl.BlockSpec(memory_space=pltpu.SMEM)
ANY = pl.BlockSpec(memory_space=pl.ANY)


def dot(a, b, ca=1, cb=0):
    return lax.dot_general(a, b, (((ca,), (cb,)), ((), ())), preferred_element_type=F32)


def shape(*dims, dtype=F32):
    return jax.ShapeDtypeStruct(dims, dtype)


def bf(*dims):
    return shape(*dims, dtype=BF16)


def call(
    kernel, outs, specs, name, cost, after=(), aliases=None, scratch=(), out_specs=None, limit=LIMIT
):
    held = len(after)
    nbytes = sum(o.size * o.dtype.itemsize for o in outs)
    run = pl.pallas_call(
        (lambda *refs: kernel(*refs[held:])) if held else kernel,
        out_shape=outs,
        in_specs=[ANY] * held + specs,
        out_specs=out_specs or [VMEM] * len(outs),
        scratch_shapes=list(scratch),
        input_output_aliases={held + i: o for i, o in (aliases or {}).items()},
        compiler_params=pltpu.CompilerParams(vmem_limit_bytes=limit * 1024 * 1024),
        cost_estimate=pl.CostEstimate(
            flops=int(cost * 1.15e9), bytes_accessed=int(2 * nbytes), transcendentals=0
        ),
        name=name,
    )
    return lambda *args: run(*after, *args)


def normed(x):
    mean = jnp.mean(x, axis=1, keepdims=True)
    spread = jnp.mean(x * x, axis=1, keepdims=True) - mean * mean
    inverse = lax.rsqrt(spread + EPSILON)
    return (x - mean) * inverse, inverse


def norm_back(upstream, xhat, inverse, gain):
    scaled = upstream * gain
    first = jnp.mean(scaled, axis=1, keepdims=True)
    second = jnp.mean(scaled * xhat, axis=1, keepdims=True)
    return inverse * (scaled - first - xhat * second)


def ln1_kernel(x_ref, g_ref, b_ref, n_ref):
    xhat, _ = normed(x_ref[...].astype(F32))
    n_ref[...] = (xhat * g_ref[...] + b_ref[...]).astype(BF16)


def mid_kernel(tok_ref, cot_ref, g_ref, b_ref, *refs):
    blocks = (len(refs) - 4) // 2
    mid_ref, n2_ref, n2t_ref, cott_ref = refs[2 * blocks :]
    acc = tok_ref[...].astype(F32)
    for j in range(blocks):
        width = refs[j].shape[0]
        acc += dot(refs[j][...], refs[blocks + j][0, 3 * width :, :], 0, 0)
    mid_ref[...] = acc
    xhat, _ = normed(acc)
    n2 = (xhat * g_ref[...] + b_ref[...]).astype(BF16)
    n2_ref[...] = n2
    n2t_ref[...] = n2.T
    cott_ref[...] = cot_ref[...].T


def mid2_kernel(
    mid_ref, branch_ref, dn2_ref, cot_ref, g_ref, out_ref, dmid_ref, datt_ref, gg_ref, bg_ref
):
    mid = mid_ref[...]
    out_ref[...] = (mid + branch_ref[...])[:U].astype(BF16)
    xhat, inverse = normed(mid)
    up = dn2_ref[...]
    dmid = cot_ref[...].astype(F32) + norm_back(up, xhat, inverse, g_ref[...])
    dmid_ref[...] = dmid
    datt_ref[...] = dmid.astype(BF16)
    gg_ref[...] = jnp.sum(up * xhat, axis=0, keepdims=True)
    bg_ref[...] = jnp.sum(up, axis=0, keepdims=True)


def final_kernel(tok_ref, dmid_ref, dn1_ref, g_ref, out_ref, gg_ref, bg_ref):
    xhat, inverse = normed(tok_ref[...].astype(F32))
    up = dn1_ref[...]
    out_ref[...] = (dmid_ref[...] + norm_back(up, xhat, inverse, g_ref[...]))[:U].astype(BF16)
    gg_ref[...] = jnp.sum(up * xhat, axis=0, keepdims=True)
    bg_ref[...] = jnp.sum(up, axis=0, keepdims=True)


def allowed_mask(place_ref, kind_ref, len_ref, offset_ref):
    unit = place_ref[2]
    kind, first, second, offset = kind_ref[unit], len_ref[unit, 0], len_ref[unit, 1], offset_ref[unit]
    start = jnp.where(kind == 1, offset, U)
    key = lax.broadcasted_iota(jnp.int32, (ROWS, 1), 0)
    query = lax.broadcasted_iota(jnp.int32, (1, ROWS), 1)
    key_upper = key >= start
    limit = jnp.where(key < U, jnp.where(key_upper, second, first), 0)
    place = jnp.where(key_upper, key - start, key)
    key_code = jnp.where(place < limit, jnp.where(key_upper, 1, 0), 2)
    query_code = jnp.where(query >= start, 1, 0)
    return key_code == query_code


def attn_fwd_kernel(place_ref, kind_ref, len_ref, offset_ref, n1_ref, w_ref, proj_ref, ho_ref, lse_ref):
    width = w_ref.shape[1] // 4
    proj = dot(w_ref[0, 0 : 3 * width, :], n1_ref[...], 1, 1)
    proj_ref[0:width, :] = (proj[0:width] * SCALE).astype(BF16)
    proj_ref[width:, :] = proj[width:].astype(BF16)
    allowed = allowed_mask(place_ref, kind_ref, len_ref, offset_ref)
    lse_ref[...] = jnp.zeros_like(lse_ref)
    for h in range(width // HEAD):
        q, k, v = (proj_ref[c * width + h * HEAD : c * width + (h + 1) * HEAD, :] for c in range(3))
        s = jnp.where(allowed, dot(k, q, 0, 0), MASKED)
        m = jnp.max(s, axis=0, keepdims=True)
        e = jnp.exp(s - m)
        total = jnp.sum(e, axis=0, keepdims=True)
        p = (e * (1.0 / total)).astype(BF16)
        ho_ref[h * HEAD : (h + 1) * HEAD, :] = dot(v, p, 1, 0).astype(BF16)
        lse_ref[h : h + 1, :] = m + jnp.log(total)


def attn_bwd_kernel(
    heads, first, hid, place_ref, kind_ref, len_ref, offset_ref, datt_ref, n1_ref, *refs
):
    proj_refs, lse_refs, ho_refs, w_refs = (refs[k * hid : (k + 1) * hid] for k in range(4))
    refs = refs[4 * hid :]
    if not first:
        dn1_in = refs[0]
        refs = refs[1:]
    dn1_ref, grad_ref, dproj_ref, w_ref = refs
    width = w_refs[0].shape[1] // 4
    allowed = allowed_mask(place_ref, kind_ref, len_ref, offset_ref)
    datt = datt_ref[...]
    for n, (r, i) in enumerate(heads):
        for k in range(3):
            w_ref[(3 * n + k) * HEAD : (3 * n + k + 1) * HEAD, :] = w_refs[r][
                0, k * width + i * HEAD : k * width + (i + 1) * HEAD, :
            ]
    wo = jnp.concatenate(
        [w_refs[r][0, 3 * width + i * HEAD : 3 * width + (i + 1) * HEAD, :] for r, i in heads]
    )
    ho = jnp.concatenate([ho_refs[r][i * HEAD : (i + 1) * HEAD, :] for r, i in heads])
    dheads = dot(wo, datt, 1, 1).astype(BF16)
    out_grad = dot(ho, datt).astype(BF16)
    for n, (r, i) in enumerate(heads):
        q, k, v = (
            proj_refs[r][c * width + i * HEAD : c * width + (i + 1) * HEAD, :] for c in range(3)
        )
        do = dheads[n * HEAD : (n + 1) * HEAD]
        s = jnp.where(allowed, dot(k, q, 0, 0), MASKED)
        p = jnp.exp(s - lse_refs[r][i : i + 1, :])
        dp = dot(v, do, 0, 0)
        delta = jnp.sum(p * dp, axis=0, keepdims=True)
        ds = (p * (dp - delta)).astype(BF16)
        base = 3 * n * HEAD
        dproj_ref[base : base + HEAD, :] = (dot(k, ds, 1, 0) * SCALE).astype(BF16)
        dproj_ref[base + HEAD : base + 2 * HEAD, :] = dot(ds, q, 1, 1).T.astype(BF16)
        dproj_ref[base + 2 * HEAD : base + 3 * HEAD, :] = dot(p.astype(BF16), do, 1, 1).T.astype(
            BF16
        )
    dproj = dproj_ref[...]
    grad = dot(dproj, n1_ref[...]).astype(BF16)
    for n, (r, i) in enumerate(heads):
        at = (n // 2, r // 2)
        grad_ref[at[0], at[1], 0 : 3 * HEAD] = grad[3 * n * HEAD : 3 * (n + 1) * HEAD]
        grad_ref[at[0], at[1], 3 * HEAD :] = out_grad[n * HEAD : (n + 1) * HEAD]
    part = dot(dproj, w_ref[...], 0, 0)
    if first:
        dn1_ref[...] = part
    else:
        dn1_ref[...] = dn1_in[...] + part


def piece_rows(place_ref, p, rows):
    piece = (place_ref[0] ^ (p // 2)) * 2 + (place_ref[1] ^ (p % 2))
    return pl.ds(pl.multiple_of(piece * rows, 16), rows)


def ffn_kernel(at, first, place_ref, n2_ref, n2t_ref, cot_ref, cott_ref, *refs):
    groups, refs = refs[: len(set(g for g, _ in at))], refs[len(set(g for g, _ in at)) :]
    if not first:
        branch_in, dn2_in = refs[:2]
        refs = refs[2:]
    branch_ref, dn2_ref, out_ref, up_ref, down_ref, grad_ref, in_sem, out_sem = refs
    d = up_ref.shape[0]
    part = d // PIECES

    def weights(t):
        cols = pl.ds(t * TILE, TILE)
        return [
            pltpu.make_async_copy(
                groups[at[p][0]].at[at[p][1], k, :, cols],
                (up_ref, down_ref)[k].at[piece_rows(place_ref, p, part), cols],
                in_sem.at[t, 2 * p + k],
            )
            for p in range(PIECES)
            for k in range(2)
        ]

    def results(t):
        cols = pl.ds(t * TILE, TILE)
        return [
            pltpu.make_async_copy(
                grad_ref.at[k, piece_rows(place_ref, p, part), cols],
                out_ref.at[p, k, :, cols],
                out_sem.at[t, 2 * p + k],
            )
            for p in range(PIECES)
            for k in range(2)
        ]

    for t in range(d // TILE):
        for c in weights(t):
            c.start()
    for t in range(d // TILE):
        cols = slice(t * TILE, (t + 1) * TILE)
        for c in weights(t):
            c.wait()
        hidden = dot(n2_ref[...], up_ref[:, cols])
        d_act = dot(cot_ref[...], down_ref[:, cols])
        cdf = 0.5 * (1.0 + lax.erf(hidden * (0.5**0.5)))
        pdf = jnp.exp(-0.5 * hidden * hidden) * 0.3989422804014327
        act = (hidden * cdf).astype(BF16)
        d_hid = (d_act * (cdf + hidden * pdf)).astype(BF16)
        b_part = dot(act, down_ref[:, cols], 1, 1)
        d_part = dot(d_hid, up_ref[:, cols], 1, 1)
        if t == 0:
            if first:
                branch_ref[...] = b_part
                dn2_ref[...] = d_part
            else:
                branch_ref[...] = branch_in[...] + b_part
                dn2_ref[...] = dn2_in[...] + d_part
        else:
            branch_ref[...] += b_part
            dn2_ref[...] += d_part
        grad_ref[0, :, cols] = dot(n2t_ref[...], d_hid).astype(BF16)
        grad_ref[1, :, cols] = dot(cott_ref[...], act).astype(BF16)
        for c in results(t):
            c.start()
    for t in range(d // TILE):
        for c in results(t):
            c.wait()


def both(a, b):
    return (a.astype(F32) + b.astype(F32)).astype(BF16)


def blocks_sum(ref):
    total = ref[0].astype(F32)
    for i in range(1, ref.shape[0]):
        total += ref[i].astype(F32)
    return total


def arrive_first_kernel(qo_ref, shared_ref, z_ref, qo_out, out_ref):
    qo_out[...] = qo_ref[...]
    out_ref[0] = shared_ref[...]
    part = z_ref.shape[1]
    for k in range(2):
        out_ref[1, k * part : (k + 1) * part, :] = z_ref[k]


def pair_kernel(a_ref, b_ref, out_ref):
    out_ref[0] = a_ref[...]
    out_ref[1] = b_ref[...]


def arrive_kernel(
    place_ref, a_ref, z2_ref, z3_ref, plain_ref, shared_ref, shared_x, b_ref, all_ref
):
    b_ref[0] = z2_ref[...]
    b_ref[1] = z3_ref[...]
    part = z2_ref.shape[1]
    for i in range(4):
        for k in range(2):
            rows = slice((2 * i + k) * part, (2 * i + k + 1) * part)
            all_ref[1, rows, :] = a_ref[i, k] if i < 2 else (z2_ref, z3_ref)[i - 2][k]
    plain = plain_ref.shape[0]
    share = shared_ref.shape[0]
    all_ref[0, :plain] = plain_ref[...]
    for i, value in enumerate((shared_ref[...], shared_x[0])):
        start = plain + (place_ref[1] ^ i) * share
        all_ref[0, pl.ds(pl.multiple_of(start, share), share), :] = value


def arrive_more_kernel(rest_ref, first_x, xs_ref, y_ref, all_ref, xs_out, y_out):
    part = rest_ref.shape[1]
    all_ref[0] = rest_ref[...]
    for k in range(2):
        all_ref[1, k] = first_x[1, k * part : (k + 1) * part, :]
    all_ref[2:4] = xs_out[...] = xs_ref[...]
    all_ref[4:6] = y_out[...] = y_ref[...]


def arrive_last_kernel(a_ref, b_ref, c_ref, all_ref):
    for i, ref in enumerate((a_ref, b_ref, c_ref)):
        all_ref[2 * i : 2 * i + 2] = ref[...]


def own_ff_kernel(mine_ref, theirs_ref, low_ref, send_ref, keep_ref):
    for p in range(PIECES):
        low_ref[p] = both(mine_ref[p, :, :LOW], theirs_ref[p, :, :LOW])
        out_ref = (keep_ref, send_ref)[p % 2]
        out_ref[p // 2] = both(mine_ref[p, :, LOW:], theirs_ref[p, :, LOW:])


def cut_pairs(ref, send_ref, keep_ref, other_ref=None):
    for z in range(ref.shape[0]):
        value = ref[z] if other_ref is None else both(ref[z], other_ref[z])
        (keep_ref, send_ref)[z % 2][z // 2] = value


def own_high_kernel(keep_ref, from_ref, zsend_ref, zkeep_ref):
    cut_pairs(keep_ref, zsend_ref, zkeep_ref, from_ref)


def own_mid_kernel(keep_ref, from_ref, near_ref, far_ref):
    near_ref[...] = both(keep_ref[0], from_ref[0])
    far_ref[...] = both(keep_ref[1], from_ref[1])


def ff_mid_kernel(keep_ref, from_ref, low_ref, low_from, send_ref, keep_out):
    high = keep_ref.shape[2]
    for z in range(keep_ref.shape[0]):
        ref = (keep_out, send_ref)[z % 2]
        ref[z // 2, :, :high] = both(keep_ref[z], from_ref[z])
        for x in range(2):
            rows = slice(high + x * LOW, high + (x + 1) * LOW)
            ref[z // 2, :, rows] = both(low_ref[2 * z + x], low_from[2 * z + x])


def ff_last_kernel(near_ref, far_from, share_ref, low_keep, low_send):
    high = share_ref.shape[1]
    total = near_ref[...].astype(F32) + far_from[...].astype(F32)
    share_ref[...] = total[:, :high].astype(BF16)
    low_keep[...] = total[:, high : high + LOW].astype(BF16)
    low_send[...] = total[:, high + LOW :].astype(BF16)


def ff_total_kernel(low_ref, low_from, near_ref, far_from, share_from, out_ref):
    out_ref[:, :LOW] = both(low_ref[...], low_from[...])
    high = near_ref[...].astype(F32) + far_from[...].astype(F32) + share_from[...].astype(F32)
    out_ref[:, LOW:] = high.astype(BF16)


def ff_join_kernel(place_ref, mine_ref, theirs_ref, up_ref, down_ref):
    part = mine_ref.shape[1]
    for i, ref in enumerate((mine_ref, theirs_ref)):
        rows = pl.ds(pl.multiple_of((place_ref[1] ^ i) * part, 16), part)
        up_ref[rows, :] = ref[0].astype(F32)
        down_ref[rows, :] = ref[1].astype(F32)


def put_vectors(ref, row, value):
    high = value.astype(BF16).astype(F32)
    rows = jnp.concatenate([high, value - high], axis=0)
    ref[row : row + 2 * VECTORS, :] = rows.astype(BF16)


def get_vectors(ref, row):
    both_parts = ref[row : row + 2 * VECTORS, :].astype(F32)
    return both_parts[:VECTORS] + both_parts[VECTORS:]


def first_sum_kernel(mine_ref, theirs_ref, own_ref, other_ref):
    for c in range(own_ref.shape[0]):
        own_ref[c] = both(mine_ref[c, 0], theirs_ref[c, 0])
        other_ref[c] = both(mine_ref[c, 1], theirs_ref[c, 1])


def halve_kernel(place_ref, own_ref, from_ref, keep_ref, send_ref):
    half = own_ref.shape[1] // 2
    for c in range(own_ref.shape[0]):
        for x, ref in enumerate((keep_ref, send_ref)):
            rows = pl.ds(pl.multiple_of((place_ref[1] ^ x) * half, half), half)
            ref[c * half : (c + 1) * half, :] = both(own_ref[c, rows, :], from_ref[c, rows, :])


def chip_sum_kernel(chunk, place_ref, vectors_ref, mine_ref, theirs_ref, *outs):
    half = mine_ref.shape[2] // 2
    for i, ref in enumerate(outs):
        x, y = i // 2, i % 2
        rows = pl.ds(pl.multiple_of((place_ref[1] ^ x) * half, half), half)
        ref[0:half, :] = both(mine_ref[0, y, rows, :], theirs_ref[chunk, y, rows, :])
        put_vectors(ref, half, vectors_ref[...])


def plane_sum_kernel(half, place_ref, *refs):
    early, late = refs[:2], refs[2:6]
    block = PIECE_ROWS
    count = early[0].shape[0] // half
    for z, ref in enumerate(refs[6:]):
        for c in range(count + 1):
            start = c % count * half + (place_ref[0] ^ z) * block
            rows = pl.ds(pl.multiple_of(start, block), block)
            total = sum(p[rows, :].astype(F32) for p in (early if c < count else late))
            ref[c * block : (c + 1) * block, :] = total.astype(BF16)
        put_vectors(ref, (count + 1) * block, sum(get_vectors(part, half) for part in late))


def qo_total_kernel(*refs):
    refs, out_ref, vec_ref = refs[:-2], refs[-2], refs[-1]
    rows = out_ref.shape[0]
    vec_ref[...] = sum(get_vectors(ref, rows) for ref in refs)
    out_ref[...] = sum(ref[0:rows, :].astype(F32) for ref in refs).astype(BF16)


def stack_kernel(vectors_ref, *refs):
    *refs, out_ref, vectors_out = refs
    vectors_out[...] = vectors_ref[...]
    for i, ref in enumerate(refs):
        out_ref[i] = ref[...]


def join_kernel(place_ref, mine_ref, mine_x, others_ref, others_x, qkv_ref, out_ref, full_ref):
    width = out_ref.shape[0]
    for x, (first, rest) in enumerate(((mine_ref, others_ref), (mine_x, others_x))):
        for z in range(rest.shape[0] + 1):
            for i in range(first.shape[0] // PIECE_ROWS):
                at_z, at_x = place_ref[0] ^ z, place_ref[1] ^ x
                row = (at_x * 2 + at_z // 2) * width + i * HEAD + at_z % 2 * PIECE_ROWS
                source = rest.at[z - 1] if z else first
                full_ref[pl.ds(pl.multiple_of(row, PIECE_ROWS), PIECE_ROWS), :] = source[
                    i * PIECE_ROWS : (i + 1) * PIECE_ROWS, :
                ].astype(F32)
    qkv_ref[...] = full_ref[: 3 * width]
    out_ref[...] = full_ref[3 * width :]


def swap(value, axis, bit):
    count = lax.axis_size(axis)
    return lax.ppermute(value, axis, [(i, i ^ bit) for i in range(count)])


def over_core(value):
    return swap(value, "hid", 1)


def over_y(value):
    return swap(value, "hid", 2)


def over_x(value):
    return swap(value, "dp", 1)


def over_z(value, step):
    return swap(value, "mod", step)


def over_x_and_y(value):
    count, hid = lax.axis_size("dp"), lax.axis_size("hid")
    pairs = [(a * hid + h, (a ^ 1) * hid + (h ^ 2)) for a in range(count) for h in range(hid)]
    return lax.ppermute(value, ("dp", "hid"), pairs)


def over_more(value):
    step = 2
    while step < lax.axis_size("dp"):
        value = (value.astype(F32) + swap(value, "dp", step).astype(F32)).astype(value.dtype)
        step *= 2
    return value


def body(
    tokens,
    cotangent,
    unit_kind,
    unit_len,
    pack_offset,
    norm1_gain,
    norm1_bias,
    qkv_weight,
    out_weight,
    norm2_gain,
    norm2_bias,
    up_weight,
    down_weight,
):
    hid = lax.axis_size("hid")
    mod = lax.axis_size("mod")
    d = tokens.shape[1]
    width = out_weight.shape[0]
    z_at, x_at = lax.axis_index("mod"), lax.axis_index("dp") & 1
    unit = (lax.axis_index("dp") * hid + lax.axis_index("hid")) * mod + z_at
    place = jnp.stack([z_at, x_at, unit])
    meta = (place, unit_kind, unit_len, pack_offset)
    tok = jnp.pad(tokens, ((0, ROWS - U), (0, 0)))
    cot = jnp.pad(cotangent, ((0, ROWS - U), (0, 0)))
    g1, b1, g2, b2 = (v[None] for v in (norm1_gain, norm1_bias, norm2_gain, norm2_bias))
    part = d // PIECES
    shard = jnp.stack([up_weight, down_weight])
    mine = lax.dynamic_slice_in_dim(shard, x_at * part, part, 1)
    rest = lax.dynamic_slice_in_dim(shard, (1 - x_at) * part, part, 1)
    qo = [jnp.concatenate([qkv_weight.reshape(3 * width, d), out_weight])[None]] + [None] * 3

    row, row16, wide16, vec = shape(ROWS, d), bf(ROWS, d), bf(d, ROWS), shape(1, d)

    proj, ho, lse = [], [], []

    def attn_fwd(j, cost, after=()):
        outs = [bf(3 * width, ROWS), bf(width, ROWS), shape(8, ROWS)]
        results = call(attn_fwd_kernel, outs, [SMEM] * 4 + [VMEM] * 2, "attn_fwd", cost, after)(
            *meta, n1, qo[j]
        )
        for kept, value in zip((proj, ho, lse), results):
            kept.append(value)

    state = []

    def ffn(pieces, after=(), cost=5.4):
        arrays = list({id(a): a for a, _ in pieces}.values())
        at = tuple((next(i for i, b in enumerate(arrays) if b is a), j) for a, j in pieces)
        *state[:], grad = call(
            functools.partial(ffn_kernel, at, not state),
            [row, row, bf(PIECES, 2, part, d)],
            [SMEM] + [VMEM] * 4 + [ANY] * len(arrays) + [VMEM] * len(state),
            "ffn",
            cost,
            after,
            {5 + len(arrays): 0, 6 + len(arrays): 1} if state else None,
            [
                pltpu.VMEM((d, d), BF16),
                pltpu.VMEM((d, d), BF16),
                pltpu.VMEM((2, d, d), BF16),
                pltpu.SemaphoreType.DMA((d // TILE, 2 * PIECES)),
                pltpu.SemaphoreType.DMA((d // TILE, 2 * PIECES)),
            ],
            [VMEM, VMEM, ANY],
        )(place, n2, n2t, cot, cott, *arrays, *state)
        return grad

    qkv_rows = qkv_weight.reshape(3 * width, d)
    shared_y = over_y(jnp.where(x_at == 0, qkv_weight[2], out_weight))
    plain_y = over_y(qkv_rows[: 2 * width])
    z1, z2, z3 = (over_z(mine, z) for z in (1, 2, 3))
    (n1,) = call(ln1_kernel, [row16], [VMEM] * 3, "ln1", 2)(tok, g1, b1)
    to_core, first = call(
        arrive_first_kernel,
        [bf(1, d, d), bf(2, width, d)],
        [VMEM] * 3,
        "arrive_first",
        1,
        [n1],
    )(qo[0], shared_y, z1)
    first_x, qo[1] = over_x(first), over_core(to_core)
    attn_fwd(0, 60, [first])
    attn_fwd(1, 60)
    (a01,) = call(pair_kernel, [bf(2, 2, part, d)], [VMEM] * 2, "pair", 1, [ho[0], ho[1]])(mine, z1)
    y01 = over_y(a01)
    a23, together = call(
        arrive_kernel,
        [bf(2, 2, part, d), bf(2, d, d)],
        [SMEM] + [VMEM] * 6,
        "arrive",
        2,
    )(place, a01, z2, z3, plain_y, shared_y, first_x)
    y23, xs = over_y(a23), over_x(a23)
    qo[2], qo[3] = together, over_core(together)
    attn_fwd(2, 60)
    attn_fwd(3, 2.4)
    mid, n2, n2t, cott = call(
        mid_kernel, [row, row16, wide16, wide16], [VMEM] * (4 + 2 * hid), "mid", 3
    )(tok, cot, g2, b2, *ho, *qo)

    to_core, xs_again, y01_again = call(
        arrive_more_kernel,
        [bf(6, 2, part, d), bf(2, 2, part, d), bf(2, 2, part, d)],
        [VMEM] * 4,
        "arrive_more",
        2,
        [mid],
    )(rest, first_x, xs, y01)
    y01x, y23x = over_x(y01_again), over_y(xs_again)
    from_core = over_core(to_core)
    b_own = qo[3].reshape(PIECES, 2, part, d)
    first_x = first_x.reshape(2, 2, part, d)
    rest = rest[None]
    f0 = ffn(
        [
            (a01, 0),
            (rest, 0),
            (a01, 1),
            (first_x, 1),
            (a23, 0),
            (xs, 0),
            (a23, 1),
            (xs, 1),
        ],
        [to_core],
        cost=60,
    )
    f1 = ffn(
        [
            (b_own, 4),
            (from_core, 0),
            (b_own, 5),
            (from_core, 1),
            (b_own, 6),
            (from_core, 2),
            (b_own, 7),
            (from_core, 3),
        ],
    )
    c1 = over_core(f1)
    (to_core,) = call(arrive_last_kernel, [bf(6, 2, part, d)], [VMEM] * 3, "arrive_last", 60, [f1])(
        y01x, y23, y23x
    )
    last = over_core(to_core)
    high = bf(mod, 2, part - LOW, d)
    halves = [bf(PIECES, 2, LOW, d), high, high]
    own_low, own_send, own_keep = call(
        own_ff_kernel, halves, [VMEM] * 2, "own_ff", 25, [to_core]
    )(f0, c1)
    own_from = over_x(own_send)
    f3 = ffn(
        [
            (from_core, 4),
            (last, 0),
            (from_core, 5),
            (last, 1),
            (last, 2),
            (last, 4),
            (last, 3),
            (last, 5),
        ],
        [own_send],
    )
    c3 = over_core(f3)
    f2 = ffn(
        [(y01, 0), (y01x, 0), (y01, 1), (y01x, 1), (y23, 0), (y23x, 0), (y23, 1), (y23x, 1)],
        cost=60,
    )
    other_low, other_send, other_keep = call(
        own_ff_kernel, halves, [VMEM] * 2, "other_ff", 2
    )(f2, c3)
    low_from, other_from = over_y(other_low), over_x(other_send)
    output, dmid, datt, g2g, b2g = call(
        mid2_kernel,
        [bf(U, d), row, row16, vec, vec],
        [VMEM] * 5,
        "mid2",
        1,
        [other_low, other_send],
    )(mid, *state, cot, g2)

    state = []

    def attn_bwd(heads, cost, after=()):
        rows = 3 * HEAD * len(heads)
        dn1, grad = call(
            functools.partial(attn_bwd_kernel, heads, not state, hid),
            [row, bf(len(heads) // 2, 2, 4 * HEAD, d)],
            [SMEM] * 4 + [VMEM] * (2 + 4 * hid + len(state)),
            "attn_bwd",
            cost,
            after,
            {6 + 4 * hid: 0} if state else None,
            [pltpu.VMEM((rows, ROWS), BF16), pltpu.VMEM((rows, d), BF16)],
        )(*meta, datt, n1, *proj, *lse, *ho, *qo, *state)
        state[:] = [dn1]
        return grad

    def stage(kernel, name, outs, *arrays, after=(), first=VMEM, cost=10):
        return call(kernel, outs, [first] + [VMEM] * (len(arrays) - 1), name, cost, after)(*arrays)

    def gather(parts, after=()):
        rows = parts[0].shape[0] // PIECE_ROWS * PIECE_ROWS
        outs = [bf(rows, d), shape(VECTORS, d)]
        value, vectors = call(
            qo_total_kernel, outs, [VMEM] * len(parts), "qo_total", 1, after
        )(*parts)
        value = over_more(value)
        return value, over_x(value), [over_z(value, z) for z in range(1, mod)], vectors

    rows = part - LOW
    half, extra = 2 * HEAD, 2 * VECTORS
    own_z, own_keep = stage(
        own_high_kernel,
        "own_high",
        [bf(mod // 2, 2, rows, d)] * 2,
        own_keep,
        own_from,
        after=[datt],
        cost=1,
    )
    own_zfrom = over_z(own_z, 1)
    count = width // HEAD
    theirs = attn_bwd([(r, i) for i in range(count) for r in (1, 3)], 20, [own_z])
    theirs = over_core(theirs)
    own_near, own_far = stage(
        own_mid_kernel, "own_mid", [bf(2, rows, d)] * 2, own_keep, own_zfrom, after=state, cost=1
    )
    own_far = over_z(own_far, 2)
    early = attn_bwd([(r, i) for i in range(count - 1) for r in (0, 2)], 60)
    own_early, other_early = stage(
        first_sum_kernel,
        "first_sum",
        [bf(count - 1, 4 * HEAD, d)] * 2,
        early,
        theirs,
    )
    early_from = over_y(other_early)
    zsend, zkeep = stage(
        ff_mid_kernel,
        "ff_mid",
        [bf(mod // 2, 2, rows + 2 * LOW, d)] * 2,
        other_keep,
        other_from,
        own_low,
        low_from,
        after=[own_early],
    )
    zfrom = over_z(zsend, 1)
    late = attn_bwd([(r, count - 1) for r in (0, 2)], 12, [zsend])
    tokens_grad, g1g, b1g = call(
        final_kernel, [bf(U, d), vec, vec], [VMEM] * 4, "final", 15, [late, own_far]
    )(tok, dmid, *state, g1)
    vectors = jnp.pad(jnp.concatenate([g1g, b1g, g2g, b2g]), ((0, VECTORS - 4), (0, 0)))
    base, *sends = stage(
        functools.partial(chip_sum_kernel, count - 1),
        "chip_sum",
        [bf(half + extra, d)] * 4,
        place,
        vectors,
        late,
        theirs,
        first=SMEM,
    )
    late = [base] + [over(v) for over, v in zip((over_y, over_x, over_x_and_y), sends)]
    early, send = stage(
        halve_kernel,
        "halve",
        [bf((count - 1) * half, d)] * 2,
        place,
        own_early,
        early_from,
        after=[base],
        first=SMEM,
    )
    early_from = over_x(send)
    near, far = stage(
        own_mid_kernel, "ff_late", [bf(2, rows + 2 * LOW, d)] * 2, zkeep, zfrom, after=[send]
    )
    far = over_z(far, 2)
    base, *sends = stage(
        functools.partial(plane_sum_kernel, half),
        "plane_sum",
        [bf(count * PIECE_ROWS + extra, d)] * mod,
        place,
        early,
        early_from,
        *late,
        after=[near],
        first=SMEM,
        cost=20,
    )
    parts = [base] + [over_z(v, z + 1) for z, v in enumerate(sends)]
    share, low_keep, low_send = stage(
        ff_last_kernel, "ff_last", [bf(2, rows, d)] + [bf(2, LOW, d)] * 2, near, far, after=[base]
    )
    share_from, low_from = over_y(share), over_x(low_send)
    mine, vectors = stage(
        qo_total_kernel,
        "qo_total",
        [bf(count * PIECE_ROWS, d), shape(VECTORS, d)],
        *parts,
        after=[share],
    )
    mine = over_more(mine)
    vectors = over_more(vectors)
    mine_x, others = over_x(mine), [over_z(mine, z) for z in range(1, mod)]
    (ff_total,) = stage(
        ff_total_kernel,
        "ff_total",
        [bf(2, part, d)],
        low_keep,
        low_from,
        own_near,
        own_far,
        share_from,
        after=[mine],
    )
    ff_total = over_more(ff_total)
    ff_rest = over_x(ff_total)
    others, vectors = stage(
        stack_kernel,
        "stack",
        [bf(mod - 1, *mine.shape), shape(VECTORS, d)],
        vectors,
        *others,
        after=[ff_total, mine_x],
    )
    others_x = over_x(others)
    vectors = vectors + over_core(vectors)
    up_grad, down_grad = stage(
        ff_join_kernel,
        "ff_join",
        [shape(2 * part, d)] * 2,
        place,
        ff_total,
        ff_rest,
        after=[others],
        first=SMEM,
    )
    qkv_grad, out_grad = call(
        join_kernel,
        [shape(3 * width, d), shape(width, d)],
        [SMEM] + [VMEM] * 4,
        "join",
        2,
        scratch=[pltpu.VMEM((d, d), F32)],
    )(place, mine, mine_x, others, others_x)
    return (
        output,
        tokens_grad,
        vectors[0],
        vectors[1],
        qkv_grad.reshape(3, width, d),
        out_grad,
        vectors[2],
        vectors[3],
        up_grad,
        down_grad,
    )


def solution(mesh):
    rows = P(("dp", "hid", "mod"), None)
    in_specs = (
        rows,
        rows,
        P(),
        P(),
        P(),
        P(),
        P(),
        P(None, "hid", None),
        P("hid", None),
        P(),
        P(),
        P("mod", "hid"),
        P("mod", "hid"),
    )
    out_specs = (
        rows,
        rows,
        P(),
        P(),
        P(None, "hid", None),
        P("hid", None),
        P(),
        P(),
        P("mod", "hid"),
        P("mod", "hid"),
    )
    return jax.shard_map(body, mesh=mesh, in_specs=in_specs, out_specs=out_specs, check_vma=False)
```

```python
import functools

import jax
import jax.numpy as jnp
from jax import lax
from jax.experimental import pallas as pl
from jax.experimental.pallas import tpu as pltpu
from jax.sharding import PartitionSpec as P

HEAD = 64
U = 529
ROWS = 544
PIECES = 8
LOW = 32
PIECE_ROWS = 32
VECTORS = 8
LIMIT = 16
TILE = 256
EPSILON = 1e-06
MASKED = -1000000000.0
SCALE = HEAD**-0.5
F32 = jnp.float32
BF16 = jnp.bfloat16
VMEM = pl.BlockSpec(memory_space=pltpu.VMEM)
SMEM = pl.BlockSpec(memory_space=pltpu.SMEM)
ANY = pl.BlockSpec(memory_space=pl.ANY)


def dot(a, b, ca=1, cb=0):
    return lax.dot_general(a, b, (((ca,), (cb,)), ((), ())), preferred_element_type=F32)


def shape(*dims, dtype=F32):
    return jax.ShapeDtypeStruct(dims, dtype)


def bf(*dims):
    return shape(*dims, dtype=BF16)


def call(
    kernel, outs, specs, name, cost, after=(), aliases=None, scratch=(), out_specs=None, limit=LIMIT
):
    held = len(after)
    nbytes = sum(o.size * o.dtype.itemsize for o in outs)
    run = pl.pallas_call(
        (lambda *refs: kernel(*refs[held:])) if held else kernel,
        out_shape=outs,
        in_specs=[ANY] * held + specs,
        out_specs=out_specs or [VMEM] * len(outs),
        scratch_shapes=list(scratch),
        input_output_aliases={held + i: o for i, o in (aliases or {}).items()},
        compiler_params=pltpu.CompilerParams(vmem_limit_bytes=limit * 1024 * 1024),
        cost_estimate=pl.CostEstimate(
            flops=int(cost * 1.15e9), bytes_accessed=int(2 * nbytes), transcendentals=0
        ),
        name=name,
    )
    return lambda *args: run(*after, *args)


def normed(x):
    mean = jnp.mean(x, axis=1, keepdims=True)
    spread = jnp.mean(x * x, axis=1, keepdims=True) - mean * mean
    inverse = lax.rsqrt(spread + EPSILON)
    return (x - mean) * inverse, inverse


def norm_back(upstream, xhat, inverse, gain):
    scaled = upstream * gain
    first = jnp.mean(scaled, axis=1, keepdims=True)
    second = jnp.mean(scaled * xhat, axis=1, keepdims=True)
    return inverse * (scaled - first - xhat * second)


def ln1_kernel(x_ref, g_ref, b_ref, n_ref):
    xhat, _ = normed(x_ref[...].astype(F32))
    n_ref[...] = (xhat * g_ref[...] + b_ref[...]).astype(BF16)


def mid_kernel(tok_ref, cot_ref, g_ref, b_ref, *refs):
    blocks = (len(refs) - 4) // 2
    mid_ref, n2_ref, n2t_ref, cott_ref = refs[2 * blocks :]
    acc = tok_ref[...].astype(F32)
    for j in range(blocks):
        width = refs[j].shape[0]
        acc += dot(refs[j][...], refs[blocks + j][0, 3 * width :, :], 0, 0)
    mid_ref[...] = acc
    xhat, _ = normed(acc)
    n2 = (xhat * g_ref[...] + b_ref[...]).astype(BF16)
    n2_ref[...] = n2
    n2t_ref[...] = n2.T
    cott_ref[...] = cot_ref[...].T


def mid2_kernel(
    mid_ref, branch_ref, dn2_ref, cot_ref, g_ref, out_ref, dmid_ref, datt_ref, gg_ref, bg_ref
):
    mid = mid_ref[...]
    out_ref[...] = (mid + branch_ref[...])[:U].astype(BF16)
    xhat, inverse = normed(mid)
    up = dn2_ref[...]
    dmid = cot_ref[...].astype(F32) + norm_back(up, xhat, inverse, g_ref[...])
    dmid_ref[...] = dmid
    datt_ref[...] = dmid.astype(BF16)
    gg_ref[...] = jnp.sum(up * xhat, axis=0, keepdims=True)
    bg_ref[...] = jnp.sum(up, axis=0, keepdims=True)


def final_kernel(tok_ref, dmid_ref, dn1_ref, g_ref, out_ref, gg_ref, bg_ref):
    xhat, inverse = normed(tok_ref[...].astype(F32))
    up = dn1_ref[...]
    out_ref[...] = (dmid_ref[...] + norm_back(up, xhat, inverse, g_ref[...]))[:U].astype(BF16)
    gg_ref[...] = jnp.sum(up * xhat, axis=0, keepdims=True)
    bg_ref[...] = jnp.sum(up, axis=0, keepdims=True)


def allowed_mask(place_ref, kind_ref, len_ref, offset_ref):
    unit = place_ref[2]
    kind, first, second, offset = kind_ref[unit], len_ref[unit, 0], len_ref[unit, 1], offset_ref[unit]
    start = jnp.where(kind == 1, offset, U)
    key = lax.broadcasted_iota(jnp.int32, (ROWS, 1), 0)
    query = lax.broadcasted_iota(jnp.int32, (1, ROWS), 1)
    key_upper = key >= start
    limit = jnp.where(key < U, jnp.where(key_upper, second, first), 0)
    place = jnp.where(key_upper, key - start, key)
    key_code = jnp.where(place < limit, jnp.where(key_upper, 1, 0), 2)
    query_code = jnp.where(query >= start, 1, 0)
    return key_code == query_code


def attn_fwd_kernel(place_ref, kind_ref, len_ref, offset_ref, n1_ref, w_ref, proj_ref, ho_ref, lse_ref):
    width = w_ref.shape[1] // 4
    proj = dot(w_ref[0, 0 : 3 * width, :], n1_ref[...], 1, 1)
    proj_ref[0:width, :] = (proj[0:width] * SCALE).astype(BF16)
    proj_ref[width:, :] = proj[width:].astype(BF16)
    allowed = allowed_mask(place_ref, kind_ref, len_ref, offset_ref)
    lse_ref[...] = jnp.zeros_like(lse_ref)
    for h in range(width // HEAD):
        q, k, v = (proj_ref[c * width + h * HEAD : c * width + (h + 1) * HEAD, :] for c in range(3))
        s = jnp.where(allowed, dot(k, q, 0, 0), MASKED)
        m = jnp.max(s, axis=0, keepdims=True)
        e = jnp.exp(s - m)
        total = jnp.sum(e, axis=0, keepdims=True)
        p = (e * (1.0 / total)).astype(BF16)
        ho_ref[h * HEAD : (h + 1) * HEAD, :] = dot(v, p, 1, 0).astype(BF16)
        lse_ref[h : h + 1, :] = m + jnp.log(total)


def attn_bwd_kernel(
    heads, first, hid, place_ref, kind_ref, len_ref, offset_ref, datt_ref, n1_ref, *refs
):
    proj_refs, lse_refs, ho_refs, w_refs = (refs[k * hid : (k + 1) * hid] for k in range(4))
    refs = refs[4 * hid :]
    if not first:
        dn1_in = refs[0]
        refs = refs[1:]
    dn1_ref, grad_ref, dproj_ref, w_ref = refs
    width = w_refs[0].shape[1] // 4
    allowed = allowed_mask(place_ref, kind_ref, len_ref, offset_ref)
    datt = datt_ref[...]
    for n, (r, i) in enumerate(heads):
        for k in range(3):
            w_ref[(3 * n + k) * HEAD : (3 * n + k + 1) * HEAD, :] = w_refs[r][
                0, k * width + i * HEAD : k * width + (i + 1) * HEAD, :
            ]
    wo = jnp.concatenate(
        [w_refs[r][0, 3 * width + i * HEAD : 3 * width + (i + 1) * HEAD, :] for r, i in heads]
    )
    ho = jnp.concatenate([ho_refs[r][i * HEAD : (i + 1) * HEAD, :] for r, i in heads])
    dheads = dot(wo, datt, 1, 1).astype(BF16)
    out_grad = dot(ho, datt).astype(BF16)
    for n, (r, i) in enumerate(heads):
        q, k, v = (
            proj_refs[r][c * width + i * HEAD : c * width + (i + 1) * HEAD, :] for c in range(3)
        )
        do = dheads[n * HEAD : (n + 1) * HEAD]
        s = jnp.where(allowed, dot(k, q, 0, 0), MASKED)
        p = jnp.exp(s - lse_refs[r][i : i + 1, :])
        dp = dot(v, do, 0, 0)
        delta = jnp.sum(p * dp, axis=0, keepdims=True)
        ds = (p * (dp - delta)).astype(BF16)
        base = 3 * n * HEAD
        dproj_ref[base : base + HEAD, :] = (dot(k, ds, 1, 0) * SCALE).astype(BF16)
        dproj_ref[base + HEAD : base + 2 * HEAD, :] = dot(ds, q, 1, 1).T.astype(BF16)
        dproj_ref[base + 2 * HEAD : base + 3 * HEAD, :] = dot(p.astype(BF16), do, 1, 1).T.astype(
            BF16
        )
    dproj = dproj_ref[...]
    grad = dot(dproj, n1_ref[...]).astype(BF16)
    for n, (r, i) in enumerate(heads):
        at = (n // 2, r // 2)
        grad_ref[at[0], at[1], 0 : 3 * HEAD] = grad[3 * n * HEAD : 3 * (n + 1) * HEAD]
        grad_ref[at[0], at[1], 3 * HEAD :] = out_grad[n * HEAD : (n + 1) * HEAD]
    part = dot(dproj, w_ref[...], 0, 0)
    if first:
        dn1_ref[...] = part
    else:
        dn1_ref[...] = dn1_in[...] + part


def piece_rows(place_ref, p, rows):
    piece = (place_ref[0] ^ (p // 2)) * 2 + (place_ref[1] ^ (p % 2))
    return pl.ds(pl.multiple_of(piece * rows, 16), rows)


def ffn_kernel(at, first, place_ref, n2_ref, n2t_ref, cot_ref, cott_ref, *refs):
    groups, refs = refs[: len(set(g for g, _ in at))], refs[len(set(g for g, _ in at)) :]
    if not first:
        branch_in, dn2_in = refs[:2]
        refs = refs[2:]
    branch_ref, dn2_ref, out_ref, up_ref, down_ref, grad_ref, in_sem, out_sem = refs
    d = up_ref.shape[0]
    part = d // PIECES

    def weights(t):
        cols = pl.ds(t * TILE, TILE)
        return [
            pltpu.make_async_copy(
                groups[at[p][0]].at[at[p][1], k, :, cols],
                (up_ref, down_ref)[k].at[piece_rows(place_ref, p, part), cols],
                in_sem.at[t, 2 * p + k],
            )
            for p in range(PIECES)
            for k in range(2)
        ]

    def results(t):
        cols = pl.ds(t * TILE, TILE)
        return [
            pltpu.make_async_copy(
                grad_ref.at[k, piece_rows(place_ref, p, part), cols],
                out_ref.at[p, k, :, cols],
                out_sem.at[t, 2 * p + k],
            )
            for p in range(PIECES)
            for k in range(2)
        ]

    for t in range(d // TILE):
        for c in weights(t):
            c.start()
    for t in range(d // TILE):
        cols = slice(t * TILE, (t + 1) * TILE)
        for c in weights(t):
            c.wait()
        hidden = dot(n2_ref[...], up_ref[:, cols])
        d_act = dot(cot_ref[...], down_ref[:, cols])
        cdf = 0.5 * (1.0 + lax.erf(hidden * (0.5**0.5)))
        pdf = jnp.exp(-0.5 * hidden * hidden) * 0.3989422804014327
        act = (hidden * cdf).astype(BF16)
        d_hid = (d_act * (cdf + hidden * pdf)).astype(BF16)
        b_part = dot(act, down_ref[:, cols], 1, 1)
        d_part = dot(d_hid, up_ref[:, cols], 1, 1)
        if t == 0:
            if first:
                branch_ref[...] = b_part
                dn2_ref[...] = d_part
            else:
                branch_ref[...] = branch_in[...] + b_part
                dn2_ref[...] = dn2_in[...] + d_part
        else:
            branch_ref[...] += b_part
            dn2_ref[...] += d_part
        grad_ref[0, :, cols] = dot(n2t_ref[...], d_hid).astype(BF16)
        grad_ref[1, :, cols] = dot(cott_ref[...], act).astype(BF16)
        for c in results(t):
            c.start()
    for t in range(d // TILE):
        for c in results(t):
            c.wait()


def both(a, b):
    return (a.astype(F32) + b.astype(F32)).astype(BF16)


def blocks_sum(ref):
    total = ref[0].astype(F32)
    for i in range(1, ref.shape[0]):
        total += ref[i].astype(F32)
    return total


def arrive_first_kernel(qo_ref, shared_ref, z_ref, qo_out, out_ref):
    qo_out[...] = qo_ref[...]
    out_ref[0] = shared_ref[...]
    part = z_ref.shape[1]
    for k in range(2):
        out_ref[1, k * part : (k + 1) * part, :] = z_ref[k]


def pair_kernel(a_ref, b_ref, out_ref):
    out_ref[0] = a_ref[...]
    out_ref[1] = b_ref[...]


def arrive_kernel(
    place_ref, a_ref, z2_ref, z3_ref, plain_ref, shared_ref, shared_x, b_ref, all_ref
):
    b_ref[0] = z2_ref[...]
    b_ref[1] = z3_ref[...]
    part = z2_ref.shape[1]
    for i in range(4):
        for k in range(2):
            rows = slice((2 * i + k) * part, (2 * i + k + 1) * part)
            all_ref[1, rows, :] = a_ref[i, k] if i < 2 else (z2_ref, z3_ref)[i - 2][k]
    plain = plain_ref.shape[0]
    share = shared_ref.shape[0]
    all_ref[0, :plain] = plain_ref[...]
    for i, value in enumerate((shared_ref[...], shared_x[0])):
        start = plain + (place_ref[1] ^ i) * share
        all_ref[0, pl.ds(pl.multiple_of(start, share), share), :] = value


def arrive_more_kernel(rest_ref, first_x, xs_ref, y_ref, all_ref, xs_out, y_out):
    part = rest_ref.shape[1]
    all_ref[0] = rest_ref[...]
    for k in range(2):
        all_ref[1, k] = first_x[1, k * part : (k + 1) * part, :]
    all_ref[2:4] = xs_out[...] = xs_ref[...]
    all_ref[4:6] = y_out[...] = y_ref[...]


def arrive_last_kernel(a_ref, b_ref, c_ref, all_ref):
    for i, ref in enumerate((a_ref, b_ref, c_ref)):
        all_ref[2 * i : 2 * i + 2] = ref[...]


def own_ff_kernel(mine_ref, theirs_ref, low_ref, send_ref, keep_ref):
    for p in range(PIECES):
        low_ref[p] = both(mine_ref[p, :, :LOW], theirs_ref[p, :, :LOW])
        out_ref = (keep_ref, send_ref)[p % 2]
        out_ref[p // 2] = both(mine_ref[p, :, LOW:], theirs_ref[p, :, LOW:])


def cut_pairs(ref, send_ref, keep_ref, other_ref=None):
    for z in range(ref.shape[0]):
        value = ref[z] if other_ref is None else both(ref[z], other_ref[z])
        (keep_ref, send_ref)[z % 2][z // 2] = value


def own_high_kernel(keep_ref, from_ref, zsend_ref, zkeep_ref):
    cut_pairs(keep_ref, zsend_ref, zkeep_ref, from_ref)


def own_mid_kernel(keep_ref, from_ref, near_ref, far_ref):
    near_ref[...] = both(keep_ref[0], from_ref[0])
    far_ref[...] = both(keep_ref[1], from_ref[1])


def ff_mid_kernel(keep_ref, from_ref, low_ref, low_from, send_ref, keep_out):
    high = keep_ref.shape[2]
    for z in range(keep_ref.shape[0]):
        ref = (keep_out, send_ref)[z % 2]
        ref[z // 2, :, :high] = both(keep_ref[z], from_ref[z])
        for x in range(2):
            rows = slice(high + x * LOW, high + (x + 1) * LOW)
            ref[z // 2, :, rows] = both(low_ref[2 * z + x], low_from[2 * z + x])


def ff_last_kernel(near_ref, far_from, share_ref, low_keep, low_send):
    high = share_ref.shape[1]
    total = near_ref[...].astype(F32) + far_from[...].astype(F32)
    share_ref[...] = total[:, :high].astype(BF16)
    low_keep[...] = total[:, high : high + LOW].astype(BF16)
    low_send[...] = total[:, high + LOW :].astype(BF16)


def ff_total_kernel(low_ref, low_from, near_ref, far_from, share_from, out_ref):
    out_ref[:, :LOW] = both(low_ref[...], low_from[...])
    high = near_ref[...].astype(F32) + far_from[...].astype(F32) + share_from[...].astype(F32)
    out_ref[:, LOW:] = high.astype(BF16)


def ff_join_kernel(place_ref, mine_ref, theirs_ref, up_ref, down_ref):
    part = mine_ref.shape[1]
    for i, ref in enumerate((mine_ref, theirs_ref)):
        rows = pl.ds(pl.multiple_of((place_ref[1] ^ i) * part, 16), part)
        up_ref[rows, :] = ref[0].astype(F32)
        down_ref[rows, :] = ref[1].astype(F32)


def put_vectors(ref, row, value):
    high = value.astype(BF16).astype(F32)
    rows = jnp.concatenate([high, value - high], axis=0)
    ref[row : row + 2 * VECTORS, :] = rows.astype(BF16)


def get_vectors(ref, row):
    both_parts = ref[row : row + 2 * VECTORS, :].astype(F32)
    return both_parts[:VECTORS] + both_parts[VECTORS:]


def first_sum_kernel(mine_ref, theirs_ref, own_ref, other_ref):
    for c in range(own_ref.shape[0]):
        own_ref[c] = both(mine_ref[c, 0], theirs_ref[c, 0])
        other_ref[c] = both(mine_ref[c, 1], theirs_ref[c, 1])


def halve_kernel(place_ref, own_ref, from_ref, keep_ref, send_ref):
    half = own_ref.shape[1] // 2
    for c in range(own_ref.shape[0]):
        for x, ref in enumerate((keep_ref, send_ref)):
            rows = pl.ds(pl.multiple_of((place_ref[1] ^ x) * half, half), half)
            ref[c * half : (c + 1) * half, :] = both(own_ref[c, rows, :], from_ref[c, rows, :])


def chip_sum_kernel(chunk, place_ref, vectors_ref, mine_ref, theirs_ref, *outs):
    half = mine_ref.shape[2] // 2
    for i, ref in enumerate(outs):
        x, y = i // 2, i % 2
        rows = pl.ds(pl.multiple_of((place_ref[1] ^ x) * half, half), half)
        ref[0:half, :] = both(mine_ref[0, y, rows, :], theirs_ref[chunk, y, rows, :])
        put_vectors(ref, half, vectors_ref[...])


def plane_sum_kernel(half, place_ref, *refs):
    early, late = refs[:2], refs[2:6]
    block = PIECE_ROWS
    count = early[0].shape[0] // half
    for z, ref in enumerate(refs[6:]):
        for c in range(count + 1):
            start = c % count * half + (place_ref[0] ^ z) * block
            rows = pl.ds(pl.multiple_of(start, block), block)
            total = sum(p[rows, :].astype(F32) for p in (early if c < count else late))
            ref[c * block : (c + 1) * block, :] = total.astype(BF16)
        put_vectors(ref, (count + 1) * block, sum(get_vectors(part, half) for part in late))


def qo_total_kernel(*refs):
    refs, out_ref, vec_ref = refs[:-2], refs[-2], refs[-1]
    rows = out_ref.shape[0]
    vec_ref[...] = sum(get_vectors(ref, rows) for ref in refs)
    out_ref[...] = sum(ref[0:rows, :].astype(F32) for ref in refs).astype(BF16)


def stack_kernel(vectors_ref, *refs):
    *refs, out_ref, vectors_out = refs
    vectors_out[...] = vectors_ref[...]
    for i, ref in enumerate(refs):
        out_ref[i] = ref[...]


def join_kernel(x, place_ref, first_ref, rest_ref, *refs):
    qkv_ref, out_ref, half_ref, sem = refs[-4:]
    width = out_ref.shape[0]
    at_x = place_ref[1] ^ x
    for z in range(rest_ref.shape[0] + 1):
        for i in range(first_ref.shape[0] // PIECE_ROWS):
            at_z = place_ref[0] ^ z
            row = at_z // 2 * width + i * HEAD + at_z % 2 * PIECE_ROWS
            source = rest_ref.at[z - 1] if z else first_ref
            half_ref[pl.ds(pl.multiple_of(row, PIECE_ROWS), PIECE_ROWS), :] = source[
                i * PIECE_ROWS : (i + 1) * PIECE_ROWS, :
            ].astype(F32)
    rows = pl.ds(pl.multiple_of(at_x * 2 * width, width), width)
    copy = pltpu.make_async_copy(half_ref.at[0:width], qkv_ref.at[rows, :], sem.at[0])
    copy.start()
    for k, ref in enumerate((qkv_ref.at[width : 2 * width], out_ref)):

        @pl.when(at_x == k)
        def _():
            second = pltpu.make_async_copy(half_ref.at[width : 2 * width], ref, sem.at[1])
            second.start()
            second.wait()

    copy.wait()


def swap(value, axis, bit):
    count = lax.axis_size(axis)
    return lax.ppermute(value, axis, [(i, i ^ bit) for i in range(count)])


def over_core(value):
    return swap(value, "hid", 1)


def over_y(value):
    return swap(value, "hid", 2)


def over_x(value):
    return swap(value, "dp", 1)


def over_z(value, step):
    return swap(value, "mod", step)


def over_x_and_y(value):
    count, hid = lax.axis_size("dp"), lax.axis_size("hid")
    pairs = [(a * hid + h, (a ^ 1) * hid + (h ^ 2)) for a in range(count) for h in range(hid)]
    return lax.ppermute(value, ("dp", "hid"), pairs)


def over_more(value):
    step = 2
    while step < lax.axis_size("dp"):
        value = (value.astype(F32) + swap(value, "dp", step).astype(F32)).astype(value.dtype)
        step *= 2
    return value


def body(
    tokens,
    cotangent,
    unit_kind,
    unit_len,
    pack_offset,
    norm1_gain,
    norm1_bias,
    qkv_weight,
    out_weight,
    norm2_gain,
    norm2_bias,
    up_weight,
    down_weight,
):
    hid = lax.axis_size("hid")
    mod = lax.axis_size("mod")
    d = tokens.shape[1]
    width = out_weight.shape[0]
    z_at, x_at = lax.axis_index("mod"), lax.axis_index("dp") & 1
    unit = (lax.axis_index("dp") * hid + lax.axis_index("hid")) * mod + z_at
    place = jnp.stack([z_at, x_at, unit])
    meta = (place, unit_kind, unit_len, pack_offset)
    tok = jnp.pad(tokens, ((0, ROWS - U), (0, 0)))
    cot = jnp.pad(cotangent, ((0, ROWS - U), (0, 0)))
    g1, b1, g2, b2 = (v[None] for v in (norm1_gain, norm1_bias, norm2_gain, norm2_bias))
    part = d // PIECES
    shard = jnp.stack([up_weight, down_weight])
    mine = lax.dynamic_slice_in_dim(shard, x_at * part, part, 1)
    rest = lax.dynamic_slice_in_dim(shard, (1 - x_at) * part, part, 1)
    qo = [jnp.concatenate([qkv_weight.reshape(3 * width, d), out_weight])[None]] + [None] * 3

    row, row16, wide16, vec = shape(ROWS, d), bf(ROWS, d), bf(d, ROWS), shape(1, d)

    proj, ho, lse = [], [], []

    def attn_fwd(j, cost, after=()):
        outs = [bf(3 * width, ROWS), bf(width, ROWS), shape(8, ROWS)]
        results = call(attn_fwd_kernel, outs, [SMEM] * 4 + [VMEM] * 2, "attn_fwd", cost, after)(
            *meta, n1, qo[j]
        )
        for kept, value in zip((proj, ho, lse), results):
            kept.append(value)

    state = []

    def ffn(pieces, after=(), cost=5.4):
        arrays = list({id(a): a for a, _ in pieces}.values())
        at = tuple((next(i for i, b in enumerate(arrays) if b is a), j) for a, j in pieces)
        *state[:], grad = call(
            functools.partial(ffn_kernel, at, not state),
            [row, row, bf(PIECES, 2, part, d)],
            [SMEM] + [VMEM] * 4 + [ANY] * len(arrays) + [VMEM] * len(state),
            "ffn",
            cost,
            after,
            {5 + len(arrays): 0, 6 + len(arrays): 1} if state else None,
            [
                pltpu.VMEM((d, d), BF16),
                pltpu.VMEM((d, d), BF16),
                pltpu.VMEM((2, d, d), BF16),
                pltpu.SemaphoreType.DMA((d // TILE, 2 * PIECES)),
                pltpu.SemaphoreType.DMA((d // TILE, 2 * PIECES)),
            ],
            [VMEM, VMEM, ANY],
        )(place, n2, n2t, cot, cott, *arrays, *state)
        return grad

    qkv_rows = qkv_weight.reshape(3 * width, d)
    shared_y = over_y(jnp.where(x_at == 0, qkv_weight[2], out_weight))
    plain_y = over_y(qkv_rows[: 2 * width])
    z1, z2, z3 = (over_z(mine, z) for z in (1, 2, 3))
    (n1,) = call(ln1_kernel, [row16], [VMEM] * 3, "ln1", 2)(tok, g1, b1)
    to_core, first = call(
        arrive_first_kernel,
        [bf(1, d, d), bf(2, width, d)],
        [VMEM] * 3,
        "arrive_first",
        1,
        [n1],
    )(qo[0], shared_y, z1)
    first_x, qo[1] = over_x(first), over_core(to_core)
    attn_fwd(0, 60, [first])
    attn_fwd(1, 60)
    (a01,) = call(pair_kernel, [bf(2, 2, part, d)], [VMEM] * 2, "pair", 1, [ho[0], ho[1]])(mine, z1)
    y01 = over_y(a01)
    a23, together = call(
        arrive_kernel,
        [bf(2, 2, part, d), bf(2, d, d)],
        [SMEM] + [VMEM] * 6,
        "arrive",
        2,
    )(place, a01, z2, z3, plain_y, shared_y, first_x)
    y23, xs = over_y(a23), over_x(a23)
    qo[2], qo[3] = together, over_core(together)
    attn_fwd(2, 60)
    attn_fwd(3, 2.4)
    mid, n2, n2t, cott = call(
        mid_kernel, [row, row16, wide16, wide16], [VMEM] * (4 + 2 * hid), "mid", 3
    )(tok, cot, g2, b2, *ho, *qo)

    to_core, xs_again, y01_again = call(
        arrive_more_kernel,
        [bf(6, 2, part, d), bf(2, 2, part, d), bf(2, 2, part, d)],
        [VMEM] * 4,
        "arrive_more",
        2,
        [mid],
    )(rest, first_x, xs, y01)
    y01x, y23x = over_x(y01_again), over_y(xs_again)
    from_core = over_core(to_core)
    b_own = qo[3].reshape(PIECES, 2, part, d)
    first_x = first_x.reshape(2, 2, part, d)
    rest = rest[None]
    f0 = ffn(
        [
            (a01, 0),
            (rest, 0),
            (a01, 1),
            (first_x, 1),
            (a23, 0),
            (xs, 0),
            (a23, 1),
            (xs, 1),
        ],
        [to_core],
        cost=60,
    )
    f1 = ffn(
        [
            (b_own, 4),
            (from_core, 0),
            (b_own, 5),
            (from_core, 1),
            (b_own, 6),
            (from_core, 2),
            (b_own, 7),
            (from_core, 3),
        ],
    )
    c1 = over_core(f1)
    (to_core,) = call(arrive_last_kernel, [bf(6, 2, part, d)], [VMEM] * 3, "arrive_last", 60, [f1])(
        y01x, y23, y23x
    )
    last = over_core(to_core)
    high = bf(mod, 2, part - LOW, d)
    halves = [bf(PIECES, 2, LOW, d), high, high]
    own_low, own_send, own_keep = call(
        own_ff_kernel, halves, [VMEM] * 2, "own_ff", 25, [to_core]
    )(f0, c1)
    own_from = over_x(own_send)
    f3 = ffn(
        [
            (from_core, 4),
            (last, 0),
            (from_core, 5),
            (last, 1),
            (last, 2),
            (last, 4),
            (last, 3),
            (last, 5),
        ],
        [own_send],
    )
    c3 = over_core(f3)
    f2 = ffn(
        [(y01, 0), (y01x, 0), (y01, 1), (y01x, 1), (y23, 0), (y23x, 0), (y23, 1), (y23x, 1)],
        cost=60,
    )
    other_low, other_send, other_keep = call(
        own_ff_kernel, halves, [VMEM] * 2, "other_ff", 2
    )(f2, c3)
    low_from, other_from = over_y(other_low), over_x(other_send)
    output, dmid, datt, g2g, b2g = call(
        mid2_kernel,
        [bf(U, d), row, row16, vec, vec],
        [VMEM] * 5,
        "mid2",
        1,
        [other_low, other_send],
    )(mid, *state, cot, g2)

    state = []

    def attn_bwd(heads, cost, after=()):
        rows = 3 * HEAD * len(heads)
        dn1, grad = call(
            functools.partial(attn_bwd_kernel, heads, not state, hid),
            [row, bf(len(heads) // 2, 2, 4 * HEAD, d)],
            [SMEM] * 4 + [VMEM] * (2 + 4 * hid + len(state)),
            "attn_bwd",
            cost,
            after,
            {6 + 4 * hid: 0} if state else None,
            [pltpu.VMEM((rows, ROWS), BF16), pltpu.VMEM((rows, d), BF16)],
        )(*meta, datt, n1, *proj, *lse, *ho, *qo, *state)
        state[:] = [dn1]
        return grad

    def stage(kernel, name, outs, *arrays, after=(), first=VMEM, cost=10):
        return call(kernel, outs, [first] + [VMEM] * (len(arrays) - 1), name, cost, after)(*arrays)

    def gather(parts, after=()):
        rows = parts[0].shape[0] // PIECE_ROWS * PIECE_ROWS
        outs = [bf(rows, d), shape(VECTORS, d)]
        value, vectors = call(
            qo_total_kernel, outs, [VMEM] * len(parts), "qo_total", 1, after
        )(*parts)
        value = over_more(value)
        return value, over_x(value), [over_z(value, z) for z in range(1, mod)], vectors

    rows = part - LOW
    half, extra = 2 * HEAD, 2 * VECTORS
    own_z, own_keep = stage(
        own_high_kernel,
        "own_high",
        [bf(mod // 2, 2, rows, d)] * 2,
        own_keep,
        own_from,
        after=[datt],
        cost=1,
    )
    own_zfrom = over_z(own_z, 1)
    count = width // HEAD
    theirs = attn_bwd([(r, i) for i in range(count) for r in (1, 3)], 20, [own_z])
    theirs = over_core(theirs)
    own_near, own_far = stage(
        own_mid_kernel, "own_mid", [bf(2, rows, d)] * 2, own_keep, own_zfrom, after=state, cost=1
    )
    own_far = over_z(own_far, 2)
    early = attn_bwd([(r, i) for i in range(count - 1) for r in (0, 2)], 60)
    own_early, other_early = stage(
        first_sum_kernel,
        "first_sum",
        [bf(count - 1, 4 * HEAD, d)] * 2,
        early,
        theirs,
    )
    early_from = over_y(other_early)
    zsend, zkeep = stage(
        ff_mid_kernel,
        "ff_mid",
        [bf(mod // 2, 2, rows + 2 * LOW, d)] * 2,
        other_keep,
        other_from,
        own_low,
        low_from,
        after=[own_early],
    )
    zfrom = over_z(zsend, 1)
    late = attn_bwd([(r, count - 1) for r in (0, 2)], 12, [zsend])
    tokens_grad, g1g, b1g = call(
        final_kernel, [bf(U, d), vec, vec], [VMEM] * 4, "final", 15, [late, own_far]
    )(tok, dmid, *state, g1)
    vectors = jnp.pad(jnp.concatenate([g1g, b1g, g2g, b2g]), ((0, VECTORS - 4), (0, 0)))
    base, *sends = stage(
        functools.partial(chip_sum_kernel, count - 1),
        "chip_sum",
        [bf(half + extra, d)] * 4,
        place,
        vectors,
        late,
        theirs,
        first=SMEM,
    )
    late = [base] + [over(v) for over, v in zip((over_y, over_x, over_x_and_y), sends)]
    early, send = stage(
        halve_kernel,
        "halve",
        [bf((count - 1) * half, d)] * 2,
        place,
        own_early,
        early_from,
        after=[base],
        first=SMEM,
    )
    early_from = over_x(send)
    near, far = stage(
        own_mid_kernel, "ff_late", [bf(2, rows + 2 * LOW, d)] * 2, zkeep, zfrom, after=[send]
    )
    far = over_z(far, 2)
    base, *sends = stage(
        functools.partial(plane_sum_kernel, half),
        "plane_sum",
        [bf(count * PIECE_ROWS + extra, d)] * mod,
        place,
        early,
        early_from,
        *late,
        after=[near],
        first=SMEM,
        cost=20,
    )
    parts = [base] + [over_z(v, z + 1) for z, v in enumerate(sends)]
    share, low_keep, low_send = stage(
        ff_last_kernel, "ff_last", [bf(2, rows, d)] + [bf(2, LOW, d)] * 2, near, far, after=[base]
    )
    share_from, low_from = over_y(share), over_x(low_send)
    mine, vectors = stage(
        qo_total_kernel,
        "qo_total",
        [bf(count * PIECE_ROWS, d), shape(VECTORS, d)],
        *parts,
        after=[share],
    )
    mine = over_more(mine)
    vectors = over_more(vectors)
    mine_x, others = over_x(mine), [over_z(mine, z) for z in range(1, mod)]
    (ff_total,) = stage(
        ff_total_kernel,
        "ff_total",
        [bf(2, part, d)],
        low_keep,
        low_from,
        own_near,
        own_far,
        share_from,
        after=[mine],
    )
    ff_total = over_more(ff_total)
    ff_rest = over_x(ff_total)
    others, vectors = stage(
        stack_kernel,
        "stack",
        [bf(mod - 1, *mine.shape), shape(VECTORS, d)],
        vectors,
        *others,
        after=[ff_total, mine_x],
    )
    others_x = over_x(others)
    vectors = vectors + over_core(vectors)
    up_grad, down_grad = stage(
        ff_join_kernel,
        "ff_join",
        [shape(2 * part, d)] * 2,
        place,
        ff_total,
        ff_rest,
        after=[others],
        first=SMEM,
    )
    def join(x, first, rest, held, after=()):
        return call(
            functools.partial(join_kernel, x),
            [shape(3 * width, d), shape(width, d)],
            [SMEM, VMEM, VMEM] + [ANY] * len(held),
            "join",
            10,
            after,
            {3: 0, 4: 1} if held else None,
            [pltpu.VMEM((2 * width, d), F32), pltpu.SemaphoreType.DMA((2,))],
            [ANY, ANY],
        )(place, first, rest, *held)

    grads = join(0, mine, others, [], [up_grad])
    qkv_grad, out_grad = join(1, mine_x, others_x, grads)
    return (
        output,
        tokens_grad,
        vectors[0],
        vectors[1],
        qkv_grad.reshape(3, width, d),
        out_grad,
        vectors[2],
        vectors[3],
        up_grad,
        down_grad,
    )


def solution(mesh):
    rows = P(("dp", "hid", "mod"), None)
    in_specs = (
        rows,
        rows,
        P(),
        P(),
        P(),
        P(),
        P(),
        P(None, "hid", None),
        P("hid", None),
        P(),
        P(),
        P("mod", "hid"),
        P("mod", "hid"),
    )
    out_specs = (
        rows,
        rows,
        P(),
        P(),
        P(None, "hid", None),
        P("hid", None),
        P(),
        P(),
        P("mod", "hid"),
        P("mod", "hid"),
    )
    return jax.shard_map(body, mesh=mesh, in_specs=in_specs, out_specs=out_specs, check_vma=False)
```
